32 devices in a mesh: ctx: 2 (over x), ep: 16 (over z, y, core).
Axes of the slice: x: 2, y: 2, z: 4, core: 2. Of those that a mesh axis runs over, the one named last changes fastest.
Arguments:
- moe_rows: bfloat16 [4096, 2048], P(('ctx', 'ep')), may hold values from -6 to 6
- expert_ids: int32 [4096, 8], P(('ctx', 'ep')), may hold values from 0 to 31, all different within a row; in each aligned block of 128 rows (0 to 127, 128 to 255, ...) at most 36 rows name the same one
- expert_gates: bfloat16 [4096, 8], P(('ctx', 'ep')), may hold values from 0.049804688 to 1
- expert_weights: bfloat16 [32, 2048, 1536], P('ep', 'ctx'), may hold values from -0.125 to 0.125
Outputs:
- expert_hidden: bfloat16 [2, 32, 16, 36, 768], P('ctx', 'ep')
The draws below stay inside these ranges and needn't reach their ends.
Inputs may be any that keep to these rules, and one draw needn't show every extreme that they name: `expert_ids`: each token names 8 different experts; in each aligned block of 128 tokens (the tokens of one device) no expert is named more than 36 times, a bound that some block reaches.
All inputs are finite; a program needn't handle non-finite values.
Results may differ from the reference program's by a relative error of at most 0.0012.
Values may be sent and summed in bfloat16 or wider, within the bound.
A program may use at most 128 MiB of HBM per device.

```python
import math
import jax
import jax.numpy as jnp
import numpy as np
from jax import lax

D = 2048
FF = 768
TOP = 8
TOK_DEV = 128
TOKENS = 4096
EXPERTS = 32
CAP = 36
N_CTX = 2
N_EP = 16


def block_scale(stream_key, dims, cuts, least, high):
    loudness = 1.0
    for dim, blocks in cuts:
        heights = jax.random.uniform(jax.random.fold_in(jax.random.fold_in(stream_key, 6), dim), (blocks,), jnp.float32, least / len(cuts), high / len(cuts))
        loudness = loudness * jnp.repeat(jnp.exp(heights), dims[dim] // blocks).reshape((-1,) + (1,) * (len(dims) - 1 - dim))
    return loudness


def shared_out(rng, own, number, rows, count, top, limit, skew):
    order = jax.random.permutation(rng, count)
    packed, ordinary = load_shares(count, rows * top, limit, skew, True), load_shares(count, rows * top, limit, skew, False)
    places = jnp.arange(count)

    def named(sizes, rotation):
        used = int((sizes > 0).sum())
        fixed = max(1, used // 4)
        passed = fixed + (places - fixed + rotation * (used - fixed)) % max(1, count - fixed)
        return jnp.zeros((count,), jnp.int32).at[order[jnp.where(places < fixed, places, passed)]].set(jnp.asarray(sizes, jnp.int32))

    sizes = jnp.where(number % 4 == 0, named(packed, number // 4), named(ordinary, number - number // 4 - 1))
    mixed = jax.random.permutation(jax.random.fold_in(own, 3), count)
    giver, sink = mixed[0:count // 2 * 2:2], mixed[1:count // 2 * 2:2]
    room = jnp.minimum(sizes[giver] - 1, limit - sizes[sink]) // 2
    room = jnp.where((giver == order[0]) | (sink == order[0]) | (sizes[sink] == 0), 0, jnp.maximum(room, 0))
    passed = jax.random.randint(jax.random.fold_in(own, 4), (count // 2,), 0, 1 << 20) % (room + 1)
    sizes = sizes.at[giver].add(-passed).at[sink].add(passed)
    members = jnp.searchsorted(jnp.cumsum(sizes), jnp.arange(rows * top), side="right").astype(jnp.int32)
    table = members.reshape(top, rows).T
    table = table[jax.random.permutation(jax.random.fold_in(own, 1), rows)]
    rotation = jax.random.randint(jax.random.fold_in(own, 2), (rows, 1), 0, top)
    return jnp.take_along_axis(table, (jnp.arange(top)[None, :] + rotation) % top, axis=1)


def load_shares(count, total, reach, skew, full):
    weights = [(1 << 20) // math.isqrt(grade ** skew) + 1 for grade in range(1, count + 1)]
    largest = reach if full else min(reach, max(-(-total // count), total * weights[0] // sum(weights)))
    least = 1 if total - largest >= count - 1 else 0
    given, surplus = [largest] + [least] * (count - 1), total - largest - least * (count - 1)
    while surplus > 0:
        movable = [i for i in range(1, count) if given[i] < largest] or [i for i in range(1, count) if given[i] < reach]
        whole, remaining = sum([weights[i] for i in movable]), surplus
        for i in movable:
            extra = min(reach - given[i], max(1, remaining * weights[i] // whole), surplus)
            given[i] = given[i] + extra
            surplus = surplus - extra
    return np.array(given)


def scatter_about(own_key, extent, deviation, bound, cuts=(), held_as=jnp.bfloat16):
    values = deviation * jax.random.normal(own_key, extent, jnp.float32)
    if cuts:
        values = values * block_scale(own_key, extent, cuts, -0.22, 0.18)
    return jnp.clip(values, -bound, bound).astype(held_as)


def setup_inputs(seed: int = 0) -> dict:
    key_list = jax.random.split(jax.random.key(seed), 5)
    moe_rows = scatter_about(key_list[0], (TOKENS, D), 1.0, 6.0, ((0, 32),))
    expert_ids_keys = jax.random.split(jax.random.fold_in(key_list[1], 1), TOKENS // TOK_DEV)
    expert_ids_turns = jax.random.permutation(jax.random.fold_in(key_list[1], 3), TOKENS // TOK_DEV)
    expert_ids = jax.vmap(lambda own, number: shared_out(jax.random.fold_in(key_list[1], 2), own, number, TOK_DEV, EXPERTS, TOP, CAP, 2))(expert_ids_keys, expert_ids_turns).reshape((TOKENS, TOP))
    expert_gates = jnp.clip(0.049804688 + 0.9501953 * jax.random.uniform(key_list[2], (TOKENS, TOP), jnp.float32) ** block_scale(key_list[2], (TOKENS, TOP), ((0, 32),), -0.2, 0.2), 0.049804688, 1.0).astype(jnp.bfloat16)
    expert_weights = scatter_about(key_list[3], (EXPERTS, D, 2 * FF), D ** -0.5, 0.125, ((0, 16), (1, 2)))
    return dict(moe_rows=moe_rows, expert_ids=expert_ids, expert_gates=expert_gates, expert_weights=expert_weights)


def place_rows(block_rows, block_ids, block_gates, experts, capacity):
    flat_ids = block_ids.reshape(-1).astype(jnp.int32)
    markers = (flat_ids[:, None] == jnp.arange(experts, dtype=jnp.int32)[None, :]).astype(jnp.int32)
    ranking = (jnp.cumsum(markers, axis=0) - markers).astype(jnp.int32)
    slot_index = jnp.sum(ranking * markers, axis=1).astype(jnp.int32)
    places = (flat_ids * capacity + slot_index).astype(jnp.int32)
    owners = (jnp.arange(flat_ids.shape[0], dtype=jnp.int32) // block_ids.shape[1]).astype(jnp.int32)
    buffer = jnp.zeros((experts * capacity, block_rows.shape[1]), block_rows.dtype).at[places].set(block_rows[owners])
    gate_buffer = jnp.zeros((experts * capacity,), block_gates.dtype).at[places].set(block_gates.reshape(-1))
    return buffer.reshape(experts, capacity, block_rows.shape[1]), gate_buffer.reshape(experts, capacity)


def place_block(block_rows, block_ids, block_gates):
    return place_rows(block_rows, block_ids, block_gates, EXPERTS, CAP)


def reference(moe_rows, expert_ids, expert_gates, expert_weights):
    block_rows = moe_rows.reshape(N_CTX, N_EP, TOK_DEV, D)
    block_ids = expert_ids.reshape(N_CTX, N_EP, TOK_DEV, TOP)
    block_gates = expert_gates.reshape(N_CTX, N_EP, TOK_DEV, TOP)

    def per_block(block_index):
        buffers, gate_buffers = jax.vmap(place_block)(block_rows[block_index], block_ids[block_index], block_gates[block_index])

        def per_expert(expert_index):
            gathered = buffers[:, expert_index].reshape(N_EP * CAP, D)
            before = jnp.dot(gathered, expert_weights[expert_index], preferred_element_type=jnp.float32)
            scaled = gate_buffers[:, expert_index].reshape(N_EP * CAP, 1).astype(jnp.float32)
            hidden = jax.nn.silu(before[:, :FF]) * before[:, FF:] * scaled
            return hidden.astype(jnp.bfloat16).reshape(N_EP, CAP, FF)

        return lax.map(per_expert, jnp.arange(EXPERTS, dtype=jnp.int32))

    return lax.map(per_block, jnp.arange(N_CTX, dtype=jnp.int32))
```

```python
import functools
import math

import jax
import jax.numpy as jnp
from jax import lax
from jax.experimental import pallas as pl
from jax.experimental.pallas import tpu as pltpu
from jax.sharding import PartitionSpec as P

FF = 768
TOP = 8
ROW_BOUND = 6.0
WEIGHT_BOUND = 0.125
META = 16
ZS = 4
CHIPS = 8


def place_rows(block_rows, block_ids, block_gates, experts, capacity):
    flat_ids = block_ids.reshape(-1)
    markers = (flat_ids[:, None] == jnp.arange(experts, dtype=jnp.int32)[None, :]).astype(jnp.int32)
    ranking = jnp.cumsum(markers, axis=0) - markers
    slot_index = jnp.sum(ranking * markers, axis=1)
    places = flat_ids * capacity + slot_index
    owners = jnp.arange(flat_ids.shape[0], dtype=jnp.int32) // block_ids.shape[1]
    buffer = (
        jnp.zeros((experts * capacity, block_rows.shape[1]), block_rows.dtype)
        .at[places]
        .set(block_rows[owners])
    )
    gate_buffer = (
        jnp.zeros((experts * capacity,), block_gates.dtype).at[places].set(block_gates.reshape(-1))
    )
    return (
        buffer.reshape(experts, capacity, block_rows.shape[1]),
        gate_buffer.reshape(experts, capacity),
    )


def project(inputs, weights):
    return jnp.einsum("sucd,udf->uscf", inputs, weights, preferred_element_type=jnp.float32)


def activate(before, gate_values):
    scaled = jnp.transpose(gate_values, (1, 0, 2)).astype(jnp.float32)[..., None]
    return (jax.nn.silu(before[..., :FF]) * before[..., FF:] * scaled).astype(jnp.bfloat16)


def general_shards(moe_rows, expert_ids, expert_gates, expert_weights):
    sources = lax.axis_size("ep")
    held_experts = expert_weights.shape[0]
    experts = sources * held_experts
    row_count = moe_rows.shape[0]
    capacity = max(2, 9 * row_count * TOP // (8 * experts))
    buffer, gate_buffer = place_rows(moe_rows, expert_ids, expert_gates, experts, capacity)
    buffer = buffer.reshape(sources, held_experts, capacity, buffer.shape[2])
    gate_buffer = gate_buffer.reshape(sources, held_experts, capacity)
    arrived, arrived_gates = (
        lax.all_to_all(buffer, "ep", split_axis=0, concat_axis=0, tiled=True),
        lax.all_to_all(gate_buffer, "ep", split_axis=0, concat_axis=0, tiled=True),
    )
    before = project(arrived, lax.all_gather(expert_weights, "ctx", axis=1, tiled=True))
    hidden = activate(before, arrived_gates)
    return hidden[None]


def chip_at_step(step, z, y):
    first, last, odd = (7 - step) // 7, step // 7, step % 2
    other = (1 - odd) * (1 - first) + last
    i = odd * ((step + 1) // 2) + (1 - odd) * (step // 2 - 1) + first - last
    mirror = z // 2
    inner = mirror * (ZS - 1 - z) + (1 - mirror) * z
    near = 1 - i // 2
    w = inner * (near * (1 - i) + (1 - near) * i) + (1 - inner) * i
    zs = mirror * (ZS - 1 - w) + (1 - mirror) * w
    ys = y + other * (1 - 2 * y)
    return zs, ys, other


def encode(p, scale):
    q = p * scale
    q2 = q * q
    q4 = q2 * q2
    q8 = q4 * q4
    return jnp.where(q < 0, -q8, q8).astype(jnp.bfloat16)


def decode(code, scale):
    v = code.astype(jnp.float32)
    size = jnp.exp(jnp.log(jnp.abs(v)) * 0.125) * (1.0 / scale)
    return jnp.where(v < 0, -size, size)


def kernel(
    cap, scale,
    rows_ref, ids_ref, gates_ref, weights_hbm, out_ref,
    blocks, weights, mine, sent, got, gate_rows,
    load_sem, weight_sem, x_send, x_recv, up_send, down_send, y_send, core_send, unit_recv,
    part_send, part_recv,
):
    tokens, width = rows_ref.shape
    half = width // 2
    held = weights_hbm.shape[0]
    c = lax.axis_index("ctx")
    e = lax.axis_index("ep")
    z, y, k = e // 4, (e // 2) % 2, e % 2
    chip = 2 * z + y
    x_peer = {"ctx": 1 - c, "ep": e}
    y_peer = {"ctx": c, "ep": 4 * z + 2 * (1 - y) + k}
    core_peer = {"ctx": c, "ep": 4 * z + 2 * y + 1 - k}
    up_peer = {"ctx": c, "ep": e + 4}
    down_peer = {"ctx": c, "ep": e - 4}
    not_top, not_bottom = z < ZS - 1, z > 0

    barrier = pltpu.get_barrier_semaphore()

    def greet(peer):
        pl.semaphore_signal(barrier, inc=1, device_id=peer, device_id_type=pl.DeviceIdType.MESH)

    greet(x_peer)
    greet(y_peer)
    greet(core_peer)

    @pl.when(not_top)
    def _():
        greet(up_peer)

    @pl.when(not_bottom)
    def _():
        greet(down_peer)

    load = pltpu.make_async_copy(
        rows_ref.at[:, pl.ds(pl.multiple_of(c * half, half), half)],
        blocks.at[chip, k, c, pl.ds(0, tokens)],
        load_sem,
    )
    load.start()
    weight_loads = [
        pltpu.make_async_copy(weights_hbm.at[j], weights.at[j], weight_sem.at[j]) for j in range(held)
    ]
    for w in weight_loads:
        w.start()

    lane = lax.broadcasted_iota(jnp.int32, (tokens, 128), 1)
    ids = ids_ref[...]
    gates = gates_ref[...].astype(jnp.float32)
    marks = jnp.zeros((tokens, 128), jnp.float32)
    gate_of = jnp.zeros((tokens, 128), jnp.float32)
    for t in range(TOP):
        same = ids[:, t : t + 1] == lane
        marks = marks + jnp.where(same, 1.0, 0.0)
        gate_of = gate_of + jnp.where(same, gates[:, t : t + 1], 0.0)
    marks, gate_of = marks.T[:32], gate_of.T[:32]
    earlier = (
        lax.broadcasted_iota(jnp.int32, (tokens, tokens), 0)
        < lax.broadcasted_iota(jnp.int32, (tokens, tokens), 1)
    )
    rank = jnp.dot(
        marks.astype(jnp.bfloat16),
        jnp.where(earlier, 1.0, 0.0).astype(jnp.bfloat16),
        preferred_element_type=jnp.float32,
    )
    slots = jnp.where(marks > 0, rank, -1.0)
    table = jnp.concatenate(
        [slots[:16], slots[16:], gate_of[:16], gate_of[16:], jnp.zeros((META, half - 512), jnp.float32)],
        axis=1,
    )
    blocks[chip, k, c, tokens:, :] = table.astype(jnp.bfloat16)

    pl.semaphore_wait(barrier, 3 + (z + ZS - 1) // ZS + (2 * ZS - 2 - z) // ZS)

    def remote(src, dst, send_sem, recv_sem, peer):
        return pltpu.make_async_remote_copy(
            src_ref=src, dst_ref=dst, send_sem=send_sem, recv_sem=recv_sem,
            device_id=peer, device_id_type=pl.DeviceIdType.MESH,
        )

    def x_rows(plane):
        return remote(
            rows_ref.at[:, pl.ds(pl.multiple_of((1 - c) * half, half), half)],
            blocks.at[chip, k, plane, pl.ds(0, tokens)],
            x_send.at[0], x_recv.at[0], x_peer,
        )

    def x_table(plane):
        return remote(
            blocks.at[chip, k, plane, pl.ds(tokens, META)],
            blocks.at[chip, k, plane, pl.ds(tokens, META)],
            x_send.at[1], x_recv.at[1], x_peer,
        )

    x_rows(c).start()
    x_table(c).start()
    load.wait()

    def unit_copy(g, core, plane, send_sem, peer):
        unit = blocks.at[g, core, plane]
        return remote(unit, unit, send_sem, unit_recv.at[(g * 2 + core) * 2 + plane], peer)

    def each_send(step, plane, act):
        zs, ys, other = chip_at_step(step, z, y)
        g = 2 * zs + ys

        @pl.when((other == 0) & not_top & (zs <= z))
        def _():
            act(unit_copy(g, k, plane, up_send.at[zs * 2 + plane], up_peer))

        @pl.when((other == 0) & not_bottom & (zs >= z))
        def _():
            act(unit_copy(g, k, plane, down_send.at[zs * 2 + plane], down_peer))

        @pl.when(other == 0)
        def _():
            act(unit_copy(g, k, plane, y_send.at[zs * 2 + plane], y_peer))

        act(unit_copy(g, k, plane, core_send.at[g * 2 + plane], core_peer))

    def part_copy(g):
        return remote(sent.at[g], got.at[g], part_send.at[g], part_recv.at[g], x_peer)

    def compute(g):
        units = [(0, 1 - c), (1, 1 - c), (0, c), (1, c)]
        x = jnp.concatenate([blocks[g, core, plane, :tokens, :] for core, plane in units], axis=0)
        pick = lax.broadcasted_iota(jnp.int32, (META, 128), 0)
        at = pl.multiple_of((e // 8) * 128, 128)
        slot_tables = [
            blocks[g, core, plane, tokens:, pl.ds(at, 128)].astype(jnp.float32) for core, plane in units
        ]
        gate_at = pl.multiple_of((e // 8) * 128 + 256, 128)
        gate_tables = [
            blocks[g, core, plane, tokens:, pl.ds(gate_at, 128)].astype(jnp.float32)
            for core, plane in units[2:]
        ]
        target = lax.broadcasted_iota(jnp.int32, (4 * cap, 4 * tokens), 0).astype(jnp.float32)
        chosen, gate_columns = [], []
        for j in range(held):
            here = pick == (e % 8) * 2 + j
            places = []
            for u, slot_table in enumerate(slot_tables):
                slot = jnp.sum(jnp.where(here, slot_table, 0.0), axis=0, keepdims=True)
                places.append(jnp.where(slot >= 0, slot + float(u * cap), -1.0))
            hot = target == jnp.concatenate(places, axis=1)
            gate_line = jnp.concatenate(
                [jnp.sum(jnp.where(here, t, 0.0), axis=0, keepdims=True) for t in gate_tables], axis=1
            )
            gate_columns.append(
                jnp.sum(
                    jnp.where(hot[2 * cap :, 2 * tokens :], gate_line, 0.0), axis=1, keepdims=True
                )
            )
            chosen.append(
                jnp.dot(
                    jnp.where(hot, 1.0, 0.0).astype(jnp.bfloat16), x, preferred_element_type=jnp.float32
                ).astype(jnp.bfloat16)
            )
        gate_rows[g] = jnp.broadcast_to(jnp.concatenate(gate_columns, axis=0), (held * 2 * cap, 128))
        step = 512
        for n in range(0, 2 * FF, step):
            parts = [
                jnp.dot(chosen[j], weights[j, :, n : n + step], preferred_element_type=jnp.float32)
                for j in range(held)
            ]
            sent[g, :, n : n + step] = encode(
                jnp.concatenate([p[: 2 * cap] for p in parts], axis=0), scale
            )
            mine[g, :, n : n + step] = jnp.concatenate([p[2 * cap :] for p in parts], axis=0)

    def work(step, carry):
        zs, ys, other = chip_at_step(step, z, y)
        g = 2 * zs + ys
        for i in range(2):
            plane = c if i == 0 else 1 - c

            @pl.when(step > 0)
            def _():
                unit_copy(g, k, plane, core_send.at[g * 2 + plane], core_peer).wait_recv()

            if i == 1:

                @pl.when(step == 0)
                def _():
                    x_rows(plane).wait_recv()
                    x_table(plane).wait_recv()

            each_send(step, plane, lambda copy: copy.start())
        for i in range(2):
            plane = c if i == 0 else 1 - c
            unit_copy(g, 1 - k, plane, core_send.at[g * 2 + plane], core_peer).wait_recv()

        @pl.when(step == 0)
        def _():
            for w in weight_loads:
                w.wait()

        compute(g)
        part_copy(g).start()
        return carry

    lax.fori_loop(0, CHIPS, work, 0)

    def finish(step, carry):
        zs, ys, _ = chip_at_step(step, z, y)
        g = 2 * zs + ys
        part_copy(g).wait_recv()
        gate_column = gate_rows[g, :, 0:1]
        first = mine[g, :, :FF] + decode(got[g, :, :FF], scale)
        second = mine[g, :, FF:] + decode(got[g, :, FF:], scale)
        hidden = first / (1.0 + jnp.exp(-first)) * second * gate_column
        for j in range(held):
            for core in range(2):
                low = (j * 2 + core) * cap
                out_ref[0, j, 2 * g + core] = hidden[low : low + cap].astype(jnp.bfloat16)
        return carry

    lax.fori_loop(0, CHIPS, finish, 0)

    def drain(step, carry):
        zs, ys, _ = chip_at_step(step, z, y)
        for plane in (c, 1 - c):
            each_send(step, plane, lambda copy: copy.wait_send())
        part_copy(2 * zs + ys).wait_send()
        return carry

    lax.fori_loop(0, CHIPS, drain, 0)
    x_rows(c).wait_send()
    x_table(c).wait_send()


def kernel_shards(moe_rows, expert_ids, expert_gates, expert_weights):
    sources = lax.axis_size("ep")
    tokens, width = moe_rows.shape
    held, half, columns = expert_weights.shape
    cap = max(2, 9 * tokens * TOP // (8 * sources * held))
    part_rows = held * 2 * cap
    scale = 2.0 ** math.floor(math.log2(49152.0 / (half * ROW_BOUND * WEIGHT_BOUND)))
    dma = pltpu.SemaphoreType.DMA
    vmem = pl.BlockSpec(memory_space=pltpu.VMEM)
    hbm = pl.BlockSpec(memory_space=pl.ANY)
    return pl.pallas_call(
        functools.partial(kernel, cap, scale),
        out_shape=jax.ShapeDtypeStruct((1, held, sources, cap, columns // 2), jnp.bfloat16),
        in_specs=[hbm, vmem, vmem, hbm],
        out_specs=vmem,
        scratch_shapes=[
            pltpu.VMEM((CHIPS, 2, 2, tokens + META, half), jnp.bfloat16),
            pltpu.VMEM((held, half, columns), jnp.bfloat16),
            pltpu.VMEM((CHIPS, part_rows, columns), jnp.float32),
            pltpu.VMEM((CHIPS, part_rows, columns), jnp.bfloat16),
            pltpu.VMEM((CHIPS, part_rows, columns), jnp.bfloat16),
            pltpu.VMEM((CHIPS, part_rows, 128), jnp.float32),
            dma,
            dma((held,)),
            dma((2,)),
            dma((2,)),
            dma((2 * ZS,)),
            dma((2 * ZS,)),
            dma((2 * ZS,)),
            dma((2 * CHIPS,)),
            dma((4 * CHIPS,)),
            dma((CHIPS,)),
            dma((CHIPS,)),
        ],
        compiler_params=pltpu.CompilerParams(
            collective_id=0, has_side_effects=True, vmem_limit_bytes=56 * 1024 * 1024
        ),
        cost_estimate=pl.CostEstimate(
            flops=2 * CHIPS * held * 4 * cap * half * columns,
            bytes_accessed=held * half * columns * 2,
            transcendentals=0,
        ),
    )(moe_rows, expert_ids, expert_gates, expert_weights)


def solution(mesh):
    in_specs = (
        P(("ctx", "ep"), None),
        P(("ctx", "ep"), None),
        P(("ctx", "ep"), None),
        P("ep", "ctx", None),
    )
    out_specs = P("ctx", "ep", None, None, None)
    fits = mesh.shape["ctx"] == 2 and mesh.shape["ep"] == 2 * CHIPS
    body = kernel_shards if fits else general_shards
    return jax.shard_map(body, mesh=mesh, in_specs=in_specs, out_specs=out_specs, check_vma=False)
```

```python
import functools
import math

import jax
import jax.numpy as jnp
from jax import lax
from jax.experimental import pallas as pl
from jax.experimental.pallas import tpu as pltpu
from jax.sharding import PartitionSpec as P

FF = 768
TOP = 8
ROW_BOUND = 6.0
WEIGHT_BOUND = 0.125
META = 16
ZS = 4
CHIPS = 8
CHUNKS = 3


def place_rows(block_rows, block_ids, block_gates, experts, capacity):
    flat_ids = block_ids.reshape(-1)
    markers = (flat_ids[:, None] == jnp.arange(experts, dtype=jnp.int32)[None, :]).astype(jnp.int32)
    ranking = jnp.cumsum(markers, axis=0) - markers
    slot_index = jnp.sum(ranking * markers, axis=1)
    places = flat_ids * capacity + slot_index
    owners = jnp.arange(flat_ids.shape[0], dtype=jnp.int32) // block_ids.shape[1]
    buffer = (
        jnp.zeros((experts * capacity, block_rows.shape[1]), block_rows.dtype)
        .at[places]
        .set(block_rows[owners])
    )
    gate_buffer = (
        jnp.zeros((experts * capacity,), block_gates.dtype).at[places].set(block_gates.reshape(-1))
    )
    return (
        buffer.reshape(experts, capacity, block_rows.shape[1]),
        gate_buffer.reshape(experts, capacity),
    )


def project(inputs, weights):
    return jnp.einsum("sucd,udf->uscf", inputs, weights, preferred_element_type=jnp.float32)


def activate(before, gate_values):
    scaled = jnp.transpose(gate_values, (1, 0, 2)).astype(jnp.float32)[..., None]
    return (jax.nn.silu(before[..., :FF]) * before[..., FF:] * scaled).astype(jnp.bfloat16)


def general_shards(moe_rows, expert_ids, expert_gates, expert_weights):
    sources = lax.axis_size("ep")
    held_experts = expert_weights.shape[0]
    experts = sources * held_experts
    row_count = moe_rows.shape[0]
    capacity = max(2, 9 * row_count * TOP // (8 * experts))
    buffer, gate_buffer = place_rows(moe_rows, expert_ids, expert_gates, experts, capacity)
    buffer = buffer.reshape(sources, held_experts, capacity, buffer.shape[2])
    gate_buffer = gate_buffer.reshape(sources, held_experts, capacity)
    arrived, arrived_gates = (
        lax.all_to_all(buffer, "ep", split_axis=0, concat_axis=0, tiled=True),
        lax.all_to_all(gate_buffer, "ep", split_axis=0, concat_axis=0, tiled=True),
    )
    before = project(arrived, lax.all_gather(expert_weights, "ctx", axis=1, tiled=True))
    hidden = activate(before, arrived_gates)
    return hidden[None]


def chip_at_step(step, z, y):
    first, last, odd = (7 - step) // 7, step // 7, step % 2
    other = (1 - odd) * (1 - first) + last
    i = odd * ((step + 1) // 2) + (1 - odd) * (step // 2 - 1) + first - last
    mirror = z // 2
    inner = mirror * (ZS - 1 - z) + (1 - mirror) * z
    near = 1 - i // 2
    w = inner * (near * (1 - i) + (1 - near) * i) + (1 - inner) * i
    zs = mirror * (ZS - 1 - w) + (1 - mirror) * w
    ys = y + other * (1 - 2 * y)
    return zs, ys, other


def encode(p, scale):
    q = p * scale
    q2 = q * q
    q4 = q2 * q2
    q8 = q4 * q4
    return jnp.where(q < 0, -q8, q8).astype(jnp.bfloat16)


def decode(code, scale):
    v = code.astype(jnp.float32)
    size = jnp.exp(jnp.log(jnp.abs(v)) * 0.125) * (1.0 / scale)
    return jnp.where(v < 0, -size, size)


def kernel(
    cap, scale,
    rows_ref, ids_ref, gates_ref, weights_hbm, out_ref,
    blocks, weights, mine, sent, got, gate_rows,
    load_sem, weight_sem, x_send, x_recv, up_send, down_send, y_send, core_send, unit_recv,
    part_send, part_recv,
):
    tokens, width = rows_ref.shape
    half = width // 2
    held = weights_hbm.shape[0]
    chunk = FF // CHUNKS
    c = lax.axis_index("ctx")
    e = lax.axis_index("ep")
    z, y, k = e // 4, (e // 2) % 2, e % 2
    chip = 2 * z + y
    x_peer = {"ctx": 1 - c, "ep": e}
    y_peer = {"ctx": c, "ep": 4 * z + 2 * (1 - y) + k}
    core_peer = {"ctx": c, "ep": 4 * z + 2 * y + 1 - k}
    up_peer = {"ctx": c, "ep": e + 4}
    down_peer = {"ctx": c, "ep": e - 4}
    not_top, not_bottom = z < ZS - 1, z > 0

    barrier = pltpu.get_barrier_semaphore()

    def greet(peer):
        pl.semaphore_signal(barrier, inc=1, device_id=peer, device_id_type=pl.DeviceIdType.MESH)

    greet(x_peer)
    greet(y_peer)
    greet(core_peer)

    @pl.when(not_top)
    def _():
        greet(up_peer)

    @pl.when(not_bottom)
    def _():
        greet(down_peer)

    load = pltpu.make_async_copy(
        rows_ref.at[:, pl.ds(pl.multiple_of(c * half, half), half)],
        blocks.at[chip, k, c, pl.ds(0, tokens)],
        load_sem,
    )
    load.start()
    weight_loads = [
        pltpu.make_async_copy(weights_hbm.at[j], weights.at[j], weight_sem.at[j]) for j in range(held)
    ]
    for w in weight_loads:
        w.start()

    expert = lax.broadcasted_iota(jnp.int32, (32, tokens), 0)
    ids = ids_ref[...]
    gates = gates_ref[...].astype(jnp.float32)
    marks = jnp.zeros((32, tokens), jnp.float32)
    gate_of = jnp.zeros((32, tokens), jnp.float32)
    for t in range(TOP):
        same = ids[t : t + 1] == expert
        marks = marks + jnp.where(same, 1.0, 0.0)
        gate_of = gate_of + jnp.where(same, gates[t : t + 1], 0.0)
    earlier = (
        lax.broadcasted_iota(jnp.int32, (tokens, tokens), 0)
        < lax.broadcasted_iota(jnp.int32, (tokens, tokens), 1)
    )
    rank = jnp.dot(
        marks.astype(jnp.bfloat16),
        jnp.where(earlier, 1.0, 0.0).astype(jnp.bfloat16),
        preferred_element_type=jnp.float32,
    )
    slots = jnp.where(marks > 0, rank, -1.0)
    table = jnp.concatenate(
        [slots[:16], slots[16:], gate_of[:16], gate_of[16:], jnp.zeros((META, half - 512), jnp.float32)],
        axis=1,
    )
    blocks[chip, k, c, tokens:, :] = table.astype(jnp.bfloat16)

    pl.semaphore_wait(barrier, 3 + (z + ZS - 1) // ZS + (2 * ZS - 2 - z) // ZS)

    def remote(src, dst, send_sem, recv_sem, peer):
        return pltpu.make_async_remote_copy(
            src_ref=src, dst_ref=dst, send_sem=send_sem, recv_sem=recv_sem,
            device_id=peer, device_id_type=pl.DeviceIdType.MESH,
        )

    def x_rows(plane):
        return remote(
            rows_ref.at[:, pl.ds(pl.multiple_of((1 - c) * half, half), half)],
            blocks.at[chip, k, plane, pl.ds(0, tokens)],
            x_send.at[0], x_recv.at[0], x_peer,
        )

    def x_table(plane):
        return remote(
            blocks.at[chip, k, plane, pl.ds(tokens, META)],
            blocks.at[chip, k, plane, pl.ds(tokens, META)],
            x_send.at[1], x_recv.at[1], x_peer,
        )

    x_rows(c).start()
    x_table(c).start()
    load.wait()

    def unit_copy(g, core, plane, send_sem, peer):
        unit = blocks.at[g, core, plane]
        return remote(unit, unit, send_sem, unit_recv.at[(g * 2 + core) * 2 + plane], peer)

    def each_send(step, plane, act):
        zs, ys, other = chip_at_step(step, z, y)
        g = 2 * zs + ys

        act(unit_copy(g, k, plane, core_send.at[g * 2 + plane], core_peer))

        @pl.when((other == 0) & not_top & (zs <= z))
        def _():
            act(unit_copy(g, k, plane, up_send.at[zs * 2 + plane], up_peer))

        @pl.when((other == 0) & not_bottom & (zs >= z))
        def _():
            act(unit_copy(g, k, plane, down_send.at[zs * 2 + plane], down_peer))

        @pl.when(other == 0)
        def _():
            act(unit_copy(g, k, plane, y_send.at[zs * 2 + plane], y_peer))

    def part_copy(g, n):
        at = g * CHUNKS + n
        return remote(sent.at[g, n], got.at[g, n], part_send.at[at], part_recv.at[at], x_peer)

    def compute(g):
        units = [(0, 1 - c), (1, 1 - c), (0, c), (1, c)]
        x = jnp.concatenate([blocks[g, core, plane, :tokens, :] for core, plane in units], axis=0)
        pick = lax.broadcasted_iota(jnp.int32, (META, 128), 0)
        at = pl.multiple_of((e // 8) * 128, 128)
        slot_tables = [
            blocks[g, core, plane, tokens:, pl.ds(at, 128)].astype(jnp.float32) for core, plane in units
        ]
        gate_at = pl.multiple_of((e // 8) * 128 + 256, 128)
        gate_tables = [
            blocks[g, core, plane, tokens:, pl.ds(gate_at, 128)].astype(jnp.float32)
            for core, plane in units[2:]
        ]
        target = lax.broadcasted_iota(jnp.int32, (4 * cap, 4 * tokens), 0).astype(jnp.float32)
        chosen, gate_columns = [], []
        for j in range(held):
            here = pick == (e % 8) * 2 + j
            places = []
            for u, slot_table in enumerate(slot_tables):
                slot = jnp.sum(jnp.where(here, slot_table, 0.0), axis=0, keepdims=True)
                places.append(jnp.where(slot >= 0, slot + float(u * cap), -1.0))
            hot = target == jnp.concatenate(places, axis=1)
            gate_line = jnp.concatenate(
                [jnp.sum(jnp.where(here, t, 0.0), axis=0, keepdims=True) for t in gate_tables], axis=1
            )
            gate_columns.append(
                jnp.sum(
                    jnp.where(hot[2 * cap :, 2 * tokens :], gate_line, 0.0), axis=1, keepdims=True
                )
            )
            chosen.append(
                jnp.dot(
                    jnp.where(hot, 1.0, 0.0).astype(jnp.bfloat16), x, preferred_element_type=jnp.float32
                ).astype(jnp.bfloat16)
            )
        gate_rows[g] = jnp.broadcast_to(jnp.concatenate(gate_columns, axis=0), (held * 2 * cap, 128))
        for n in range(CHUNKS):
            for side in range(2):
                columns = slice(side * FF + n * chunk, side * FF + (n + 1) * chunk)
                parts = [
                    jnp.dot(chosen[j], weights[j, :, columns], preferred_element_type=jnp.float32)
                    for j in range(held)
                ]
                here = slice(side * chunk, (side + 1) * chunk)
                sent[g, n, :, here] = encode(
                    jnp.concatenate([p[: 2 * cap] for p in parts], axis=0), scale
                )
                mine[g, n, :, here] = jnp.concatenate([p[2 * cap :] for p in parts], axis=0)
            part_copy(g, n).start()

    def work(step, carry):
        zs, ys, other = chip_at_step(step, z, y)
        g = 2 * zs + ys
        for i in range(2):
            plane = c if i == 0 else 1 - c

            @pl.when(step > 0)
            def _():
                unit_copy(g, k, plane, core_send.at[g * 2 + plane], core_peer).wait_recv()

            if i == 1:

                @pl.when(step == 0)
                def _():
                    x_rows(plane).wait_recv()
                    x_table(plane).wait_recv()

            each_send(step, plane, lambda copy: copy.start())
        for i in range(2):
            plane = c if i == 0 else 1 - c
            unit_copy(g, 1 - k, plane, core_send.at[g * 2 + plane], core_peer).wait_recv()

        @pl.when(step == 0)
        def _():
            for w in weight_loads:
                w.wait()

        compute(g)
        return carry

    lax.fori_loop(0, CHIPS, work, 0)

    def finish(step, carry):
        zs, ys, _ = chip_at_step(step, z, y)
        g = 2 * zs + ys
        gate_column = gate_rows[g, :, 0:1]
        for n in range(CHUNKS):
            part_copy(g, n).wait_recv()
            first = mine[g, n, :, :chunk] + decode(got[g, n, :, :chunk], scale)
            second = mine[g, n, :, chunk:] + decode(got[g, n, :, chunk:], scale)
            hidden = first / (1.0 + jnp.exp(-first)) * second * gate_column
            for j in range(held):
                for core in range(2):
                    low = (j * 2 + core) * cap
                    out_ref[0, j, 2 * g + core, :, n * chunk : (n + 1) * chunk] = hidden[
                        low : low + cap
                    ].astype(jnp.bfloat16)
        return carry

    lax.fori_loop(0, CHIPS, finish, 0)

    def drain(step, carry):
        zs, ys, _ = chip_at_step(step, z, y)
        for plane in (c, 1 - c):
            each_send(step, plane, lambda copy: copy.wait_send())
        for n in range(CHUNKS):
            part_copy(2 * zs + ys, n).wait_send()
        return carry

    lax.fori_loop(0, CHIPS, drain, 0)
    x_rows(c).wait_send()
    x_table(c).wait_send()


def kernel_shards(moe_rows, expert_ids, expert_gates, expert_weights):
    sources = lax.axis_size("ep")
    tokens, width = moe_rows.shape
    held, half, columns = expert_weights.shape
    cap = max(2, 9 * tokens * TOP // (8 * sources * held))
    part_rows = held * 2 * cap
    scale = 2.0 ** math.floor(math.log2(49152.0 / (half * ROW_BOUND * WEIGHT_BOUND)))
    dma = pltpu.SemaphoreType.DMA
    vmem = pl.BlockSpec(memory_space=pltpu.VMEM)
    hbm = pl.BlockSpec(memory_space=pl.ANY)
    return pl.pallas_call(
        functools.partial(kernel, cap, scale),
        out_shape=pltpu.VMEM((1, held, sources, cap, columns // 2), jnp.bfloat16),
        in_specs=[hbm, vmem, vmem, hbm],
        out_specs=vmem,
        scratch_shapes=[
            pltpu.VMEM((CHIPS, 2, 2, tokens + META, half), jnp.bfloat16),
            pltpu.VMEM((held, half, columns), jnp.bfloat16),
            pltpu.VMEM((CHIPS, CHUNKS, part_rows, columns // CHUNKS), jnp.float32),
            pltpu.VMEM((CHIPS, CHUNKS, part_rows, columns // CHUNKS), jnp.bfloat16),
            pltpu.VMEM((CHIPS, CHUNKS, part_rows, columns // CHUNKS), jnp.bfloat16),
            pltpu.VMEM((CHIPS, part_rows, 128), jnp.float32),
            dma,
            dma((held,)),
            dma((2,)),
            dma((2,)),
            dma((2 * ZS,)),
            dma((2 * ZS,)),
            dma((2 * ZS,)),
            dma((2 * CHIPS,)),
            dma((4 * CHIPS,)),
            dma((CHIPS * CHUNKS,)),
            dma((CHIPS * CHUNKS,)),
        ],
        compiler_params=pltpu.CompilerParams(
            collective_id=0, has_side_effects=True, vmem_limit_bytes=56 * 1024 * 1024
        ),
        cost_estimate=pl.CostEstimate(
            flops=2 * CHIPS * held * 4 * cap * half * columns,
            bytes_accessed=held * half * columns * 2,
            transcendentals=0,
        ),
    )(moe_rows, expert_ids.T, expert_gates.T, expert_weights)


def solution(mesh):
    in_specs = (
        P(("ctx", "ep"), None),
        P(("ctx", "ep"), None),
        P(("ctx", "ep"), None),
        P("ep", "ctx", None),
    )
    out_specs = P("ctx", "ep", None, None, None)
    fits = mesh.shape["ctx"] == 2 and mesh.shape["ep"] == 2 * CHIPS
    body = kernel_shards if fits else general_shards
    return jax.shard_map(body, mesh=mesh, in_specs=in_specs, out_specs=out_specs, check_vma=False)
```

```python
import functools
import math

import jax
import jax.numpy as jnp
from jax import lax
from jax.experimental import pallas as pl
from jax.experimental.pallas import tpu as pltpu
from jax.sharding import PartitionSpec as P

FF = 768
TOP = 8
ROW_BOUND = 6.0
WEIGHT_BOUND = 0.125
META = 16
ZS = 4
CHIPS = 8
CHUNKS = 6


def place_rows(block_rows, block_ids, block_gates, experts, capacity):
    flat_ids = block_ids.reshape(-1)
    markers = (flat_ids[:, None] == jnp.arange(experts, dtype=jnp.int32)[None, :]).astype(jnp.int32)
    ranking = jnp.cumsum(markers, axis=0) - markers
    slot_index = jnp.sum(ranking * markers, axis=1)
    places = flat_ids * capacity + slot_index
    owners = jnp.arange(flat_ids.shape[0], dtype=jnp.int32) // block_ids.shape[1]
    buffer = (
        jnp.zeros((experts * capacity, block_rows.shape[1]), block_rows.dtype)
        .at[places]
        .set(block_rows[owners])
    )
    gate_buffer = (
        jnp.zeros((experts * capacity,), block_gates.dtype).at[places].set(block_gates.reshape(-1))
    )
    return (
        buffer.reshape(experts, capacity, block_rows.shape[1]),
        gate_buffer.reshape(experts, capacity),
    )


def project(inputs, weights):
    return jnp.einsum("sucd,udf->uscf", inputs, weights, preferred_element_type=jnp.float32)


def activate(before, gate_values):
    scaled = jnp.transpose(gate_values, (1, 0, 2)).astype(jnp.float32)[..., None]
    return (jax.nn.silu(before[..., :FF]) * before[..., FF:] * scaled).astype(jnp.bfloat16)


def general_shards(moe_rows, expert_ids, expert_gates, expert_weights):
    sources = lax.axis_size("ep")
    held_experts = expert_weights.shape[0]
    experts = sources * held_experts
    row_count = moe_rows.shape[0]
    capacity = max(2, 9 * row_count * TOP // (8 * experts))
    buffer, gate_buffer = place_rows(moe_rows, expert_ids, expert_gates, experts, capacity)
    buffer = buffer.reshape(sources, held_experts, capacity, buffer.shape[2])
    gate_buffer = gate_buffer.reshape(sources, held_experts, capacity)
    arrived, arrived_gates = (
        lax.all_to_all(buffer, "ep", split_axis=0, concat_axis=0, tiled=True),
        lax.all_to_all(gate_buffer, "ep", split_axis=0, concat_axis=0, tiled=True),
    )
    before = project(arrived, lax.all_gather(expert_weights, "ctx", axis=1, tiled=True))
    hidden = activate(before, arrived_gates)
    return hidden[None]


def chip_at_step(step, z, y):
    first, last, odd = (7 - step) // 7, step // 7, step % 2
    other = (1 - odd) * (1 - first) + last
    i = odd * ((step + 1) // 2) + (1 - odd) * (step // 2 - 1) + first - last
    mirror = z // 2
    inner = mirror * (ZS - 1 - z) + (1 - mirror) * z
    near = 1 - i // 2
    w = inner * (near * (1 - i) + (1 - near) * i) + (1 - inner) * i
    zs = mirror * (ZS - 1 - w) + (1 - mirror) * w
    ys = y + other * (1 - 2 * y)
    return zs, ys, other


def encode(p, scale):
    q = p * scale
    q2 = q * q
    q4 = q2 * q2
    q8 = q4 * q4
    return jnp.where(q < 0, -q8, q8).astype(jnp.bfloat16)


def decode(code, scale):
    v = code.astype(jnp.float32)
    size = jnp.exp(jnp.log(jnp.abs(v)) * 0.125) * (1.0 / scale)
    return jnp.where(v < 0, -size, size)


def kernel(
    cap, scale,
    rows_ref, ids_ref, gates_ref, weights_hbm, out_ref,
    blocks, weights, mine, sent, got, gate_rows,
    load_sem, weight_sem, x_send, x_recv, up_send, down_send, y_send, core_send, unit_recv,
    part_send, part_recv,
):
    tokens, width = rows_ref.shape
    half = width // 2
    held = weights_hbm.shape[0]
    chunk = FF // CHUNKS
    c = lax.axis_index("ctx")
    e = lax.axis_index("ep")
    z, y, k = e // 4, (e // 2) % 2, e % 2
    chip = 2 * z + y
    x_peer = {"ctx": 1 - c, "ep": e}
    y_peer = {"ctx": c, "ep": 4 * z + 2 * (1 - y) + k}
    core_peer = {"ctx": c, "ep": 4 * z + 2 * y + 1 - k}
    up_peer = {"ctx": c, "ep": e + 4}
    down_peer = {"ctx": c, "ep": e - 4}
    not_top, not_bottom = z < ZS - 1, z > 0

    barrier = pltpu.get_barrier_semaphore()

    def greet(peer):
        pl.semaphore_signal(barrier, inc=1, device_id=peer, device_id_type=pl.DeviceIdType.MESH)

    greet(x_peer)
    greet(y_peer)
    greet(core_peer)

    @pl.when(not_top)
    def _():
        greet(up_peer)

    @pl.when(not_bottom)
    def _():
        greet(down_peer)

    load = pltpu.make_async_copy(
        rows_ref.at[:, pl.ds(pl.multiple_of(c * half, half), half)],
        blocks.at[chip, k, c, pl.ds(0, tokens)],
        load_sem,
    )
    load.start()
    weight_loads = [
        pltpu.make_async_copy(
            weights_hbm.at[j, :, pl.ds(side * FF + n * chunk, chunk)],
            weights.at[n, j, :, pl.ds(side * chunk, chunk)],
            weight_sem.at[(n * held + j) * 2 + side],
        )
        for n in range(CHUNKS)
        for j in range(held)
        for side in range(2)
    ]
    for w in weight_loads:
        w.start()

    expert = lax.broadcasted_iota(jnp.int32, (32, tokens), 0)
    ids = ids_ref[...]
    gates = gates_ref[...].astype(jnp.float32)
    marks = jnp.zeros((32, tokens), jnp.float32)
    gate_of = jnp.zeros((32, tokens), jnp.float32)
    for t in range(TOP):
        same = ids[t : t + 1] == expert
        marks = marks + jnp.where(same, 1.0, 0.0)
        gate_of = gate_of + jnp.where(same, gates[t : t + 1], 0.0)
    earlier = (
        lax.broadcasted_iota(jnp.int32, (tokens, tokens), 0)
        < lax.broadcasted_iota(jnp.int32, (tokens, tokens), 1)
    )
    rank = jnp.dot(
        marks.astype(jnp.bfloat16),
        jnp.where(earlier, 1.0, 0.0).astype(jnp.bfloat16),
        preferred_element_type=jnp.float32,
    )
    slots = jnp.where(marks > 0, rank, -1.0)
    table = jnp.concatenate(
        [slots[:16], slots[16:], gate_of[:16], gate_of[16:], jnp.zeros((META, half - 512), jnp.float32)],
        axis=1,
    )
    blocks[chip, k, c, tokens:, :] = table.astype(jnp.bfloat16)
    blocks[chip, k, 1 - c, tokens:, 512:] = jnp.zeros((META, half - 512), jnp.bfloat16)

    pl.semaphore_wait(barrier, 3 + (z + ZS - 1) // ZS + (2 * ZS - 2 - z) // ZS)

    def remote(src, dst, send_sem, recv_sem, peer):
        return pltpu.make_async_remote_copy(
            src_ref=src, dst_ref=dst, send_sem=send_sem, recv_sem=recv_sem,
            device_id=peer, device_id_type=pl.DeviceIdType.MESH,
        )

    def x_rows(plane):
        return remote(
            rows_ref.at[:, pl.ds(pl.multiple_of((1 - c) * half, half), half)],
            blocks.at[chip, k, plane, pl.ds(0, tokens)],
            x_send.at[0], x_recv.at[0], x_peer,
        )

    def x_table(plane):
        return remote(
            blocks.at[chip, k, plane, pl.ds(tokens, META), pl.ds(0, 512)],
            blocks.at[chip, k, plane, pl.ds(tokens, META), pl.ds(0, 512)],
            x_send.at[1], x_recv.at[1], x_peer,
        )

    x_rows(c).start()
    x_table(c).start()
    load.wait()

    def unit_copy(g, core, plane, send_sem, peer):
        unit = blocks.at[g, core, plane]
        return remote(unit, unit, send_sem, unit_recv.at[(g * 2 + core) * 2 + plane], peer)

    def each_send(step, plane, act):
        zs, ys, other = chip_at_step(step, z, y)
        g = 2 * zs + ys

        act(unit_copy(g, k, plane, core_send.at[g * 2 + plane], core_peer))

        @pl.when((other == 0) & not_top & (zs <= z))
        def _():
            act(unit_copy(g, k, plane, up_send.at[zs * 2 + plane], up_peer))

        @pl.when((other == 0) & not_bottom & (zs >= z))
        def _():
            act(unit_copy(g, k, plane, down_send.at[zs * 2 + plane], down_peer))

        @pl.when(other == 0)
        def _():
            act(unit_copy(g, k, plane, y_send.at[zs * 2 + plane], y_peer))

    def part_copy(g, n):
        at = g * CHUNKS + n
        return remote(sent.at[g, n], got.at[g, n], part_send.at[at], part_recv.at[at], x_peer)

    def place(g, plane, gates_too):
        x = jnp.concatenate([blocks[g, core, plane, :tokens, :] for core in range(2)], axis=0)
        pick = lax.broadcasted_iota(jnp.int32, (META, 128), 0)
        row = lax.broadcasted_iota(jnp.int32, (2 * cap, 2 * tokens), 0).astype(jnp.float32)

        def lines(first, j):
            at = pl.multiple_of((e // 8) * 128 + first, 128)
            return [
                jnp.sum(
                    jnp.where(
                        pick == (e % 8) * 2 + j,
                        blocks[g, core, plane, tokens:, pl.ds(at, 128)].astype(jnp.float32),
                        0.0,
                    ),
                    axis=0,
                    keepdims=True,
                )
                for core in range(2)
            ]

        hots, gate_columns = [], []
        for j in range(held):
            near, far = lines(0, j)
            far = jnp.where(far >= 0, far + float(cap), -1.0)
            hot = row == jnp.concatenate([near, far], axis=1)
            hots.append(jnp.where(hot, 1.0, 0.0))
            if gates_too:
                gate_line = jnp.concatenate(lines(256, j), axis=1)
                gate_columns.append(jnp.sum(jnp.where(hot, gate_line, 0.0), axis=1, keepdims=True))
        if gates_too:
            column = jnp.concatenate(gate_columns, axis=0)
            gate_rows[g] = jnp.broadcast_to(column, (held * 2 * cap, 128))
        return jnp.dot(
            jnp.concatenate(hots, axis=0).astype(jnp.bfloat16), x, preferred_element_type=jnp.float32
        )

    def compute(g, theirs, ours):
        rows = [slice(j * 2 * cap, (j + 1) * 2 * cap) for j in range(held)]
        chosen = [
            jnp.concatenate([theirs[r], ours[r]], axis=0).astype(jnp.bfloat16) for r in rows
        ]
        for n in range(CHUNKS):
            parts = [
                jnp.dot(chosen[j], weights[n, j], preferred_element_type=jnp.float32)
                for j in range(held)
            ]
            sent[g, n] = encode(jnp.concatenate([p[: 2 * cap] for p in parts], axis=0), scale)
            part_copy(g, n).start()
            mine[g, n] = jnp.concatenate([p[2 * cap :] for p in parts], axis=0)

    def work(step, carry):
        zs, ys, other = chip_at_step(step, z, y)
        g = 2 * zs + ys

        @pl.when(step > 0)
        def _():
            unit_copy(g, k, c, core_send.at[g * 2 + c], core_peer).wait_recv()

        each_send(step, c, lambda copy: copy.start())
        unit_copy(g, 1 - k, c, core_send.at[g * 2 + c], core_peer).wait_recv()
        ours = place(g, c, True)

        @pl.when(step == 0)
        def _():
            for w in weight_loads:
                w.wait()
            x_rows(1 - c).wait_recv()
            x_table(1 - c).wait_recv()

        @pl.when(step > 0)
        def _():
            unit_copy(g, k, 1 - c, core_send.at[g * 2 + 1 - c], core_peer).wait_recv()

        each_send(step, 1 - c, lambda copy: copy.start())
        unit_copy(g, 1 - k, 1 - c, core_send.at[g * 2 + 1 - c], core_peer).wait_recv()
        compute(g, place(g, 1 - c, False), ours)
        return carry

    lax.fori_loop(0, CHIPS, work, 0)

    def finish(step, carry):
        zs, ys, _ = chip_at_step(step, z, y)
        g = 2 * zs + ys
        gate_column = gate_rows[g, :, 0:1]
        for plane in (c, 1 - c):
            each_send(step, plane, lambda copy: copy.wait_send())
        for n in range(CHUNKS):
            part_copy(g, n).wait_recv()
            first = mine[g, n, :, :chunk] + decode(got[g, n, :, :chunk], scale)
            second = mine[g, n, :, chunk:] + decode(got[g, n, :, chunk:], scale)
            hidden = first / (1.0 + jnp.exp(-first)) * second * gate_column
            for j in range(held):
                for core in range(2):
                    low = (j * 2 + core) * cap
                    out_ref[0, j, 2 * g + core, :, n * chunk : (n + 1) * chunk] = hidden[
                        low : low + cap
                    ].astype(jnp.bfloat16)
            part_copy(g, n).wait_send()
        return carry

    x_rows(c).wait_send()
    x_table(c).wait_send()
    lax.fori_loop(0, CHIPS, finish, 0)


def kernel_shards(moe_rows, expert_ids, expert_gates, expert_weights):
    sources = lax.axis_size("ep")
    tokens, width = moe_rows.shape
    held, half, columns = expert_weights.shape
    cap = max(2, 9 * tokens * TOP // (8 * sources * held))
    part_rows = held * 2 * cap
    scale = 2.0 ** math.floor(math.log2(49152.0 / (half * ROW_BOUND * WEIGHT_BOUND)))
    dma = pltpu.SemaphoreType.DMA
    vmem = pl.BlockSpec(memory_space=pltpu.VMEM)
    hbm = pl.BlockSpec(memory_space=pl.ANY)
    return pl.pallas_call(
        functools.partial(kernel, cap, scale),
        out_shape=pltpu.VMEM((1, held, sources, cap, columns // 2), jnp.bfloat16),
        in_specs=[hbm, vmem, vmem, hbm],
        out_specs=vmem,
        scratch_shapes=[
            pltpu.VMEM((CHIPS, 2, 2, tokens + META, half), jnp.bfloat16),
            pltpu.VMEM((CHUNKS, held, half, columns // CHUNKS), jnp.bfloat16),
            pltpu.VMEM((CHIPS, CHUNKS, part_rows, columns // CHUNKS), jnp.float32),
            pltpu.VMEM((CHIPS, CHUNKS, part_rows, columns // CHUNKS), jnp.bfloat16),
            pltpu.VMEM((CHIPS, CHUNKS, part_rows, columns // CHUNKS), jnp.bfloat16),
            pltpu.VMEM((CHIPS, part_rows, 128), jnp.float32),
            dma,
            dma((CHUNKS * held * 2,)),
            dma((2,)),
            dma((2,)),
            dma((2 * ZS,)),
            dma((2 * ZS,)),
            dma((2 * ZS,)),
            dma((2 * CHIPS,)),
            dma((4 * CHIPS,)),
            dma((CHIPS * CHUNKS,)),
            dma((CHIPS * CHUNKS,)),
        ],
        compiler_params=pltpu.CompilerParams(
            collective_id=0, has_side_effects=True, vmem_limit_bytes=56 * 1024 * 1024
        ),
        cost_estimate=pl.CostEstimate(
            flops=2 * CHIPS * held * 4 * cap * half * columns,
            bytes_accessed=held * half * columns * 2,
            transcendentals=0,
        ),
    )(moe_rows, expert_ids.T, expert_gates.T, expert_weights)


def solution(mesh):
    in_specs = (
        P(("ctx", "ep"), None),
        P(("ctx", "ep"), None),
        P(("ctx", "ep"), None),
        P("ep", "ctx", None),
    )
    out_specs = P("ctx", "ep", None, None, None)
    fits = mesh.shape["ctx"] == 2 and mesh.shape["ep"] == 2 * CHIPS
    body = kernel_shards if fits else general_shards
    return jax.shard_map(body, mesh=mesh, in_specs=in_specs, out_specs=out_specs, check_vma=False)
```

```python
import functools
import math

import jax
import jax.numpy as jnp
from jax import lax
from jax.experimental import pallas as pl
from jax.experimental.pallas import tpu as pltpu
from jax.sharding import PartitionSpec as P

FF = 768
TOP = 8
ROW_BOUND = 6.0
WEIGHT_BOUND = 0.125
META = 16
ZS = 4
CHIPS = 8
CHUNKS = 3


def place_rows(block_rows, block_ids, block_gates, experts, capacity):
    flat_ids = block_ids.reshape(-1)
    markers = (flat_ids[:, None] == jnp.arange(experts, dtype=jnp.int32)[None, :]).astype(jnp.int32)
    ranking = jnp.cumsum(markers, axis=0) - markers
    slot_index = jnp.sum(ranking * markers, axis=1)
    places = flat_ids * capacity + slot_index
    owners = jnp.arange(flat_ids.shape[0], dtype=jnp.int32) // block_ids.shape[1]
    buffer = (
        jnp.zeros((experts * capacity, block_rows.shape[1]), block_rows.dtype)
        .at[places]
        .set(block_rows[owners])
    )
    gate_buffer = (
        jnp.zeros((experts * capacity,), block_gates.dtype).at[places].set(block_gates.reshape(-1))
    )
    return (
        buffer.reshape(experts, capacity, block_rows.shape[1]),
        gate_buffer.reshape(experts, capacity),
    )


def project(inputs, weights):
    return jnp.einsum("sucd,udf->uscf", inputs, weights, preferred_element_type=jnp.float32)


def activate(before, gate_values):
    scaled = jnp.transpose(gate_values, (1, 0, 2)).astype(jnp.float32)[..., None]
    return (jax.nn.silu(before[..., :FF]) * before[..., FF:] * scaled).astype(jnp.bfloat16)


def general_shards(moe_rows, expert_ids, expert_gates, expert_weights):
    sources = lax.axis_size("ep")
    held_experts = expert_weights.shape[0]
    experts = sources * held_experts
    row_count = moe_rows.shape[0]
    capacity = max(2, 9 * row_count * TOP // (8 * experts))
    buffer, gate_buffer = place_rows(moe_rows, expert_ids, expert_gates, experts, capacity)
    buffer = buffer.reshape(sources, held_experts, capacity, buffer.shape[2])
    gate_buffer = gate_buffer.reshape(sources, held_experts, capacity)
    arrived, arrived_gates = (
        lax.all_to_all(buffer, "ep", split_axis=0, concat_axis=0, tiled=True),
        lax.all_to_all(gate_buffer, "ep", split_axis=0, concat_axis=0, tiled=True),
    )
    before = project(arrived, lax.all_gather(expert_weights, "ctx", axis=1, tiled=True))
    hidden = activate(before, arrived_gates)
    return hidden[None]


def chip_at_step(step, z, y):
    first, last, odd = (7 - step) // 7, step // 7, step % 2
    other = (1 - odd) * (1 - first) + last
    i = odd * ((step + 1) // 2) + (1 - odd) * (step // 2 - 1) + first - last
    mirror = z // 2
    inner = mirror * (ZS - 1 - z) + (1 - mirror) * z
    near = 1 - i // 2
    w = inner * (near * (1 - i) + (1 - near) * i) + (1 - inner) * i
    zs = mirror * (ZS - 1 - w) + (1 - mirror) * w
    ys = y + other * (1 - 2 * y)
    return zs, ys, other


def encode(p, scale):
    q = p * scale
    q2 = q * q
    q4 = q2 * q2
    q8 = q4 * q4
    return jnp.where(q < 0, -q8, q8).astype(jnp.bfloat16)


def decode(code, scale):
    v = code.astype(jnp.float32)
    size = jnp.exp(jnp.log(jnp.abs(v)) * 0.125) * (1.0 / scale)
    return jnp.where(v < 0, -size, size)


def kernel(
    cap, scale,
    rows_ref, ids_ref, gates_ref, weights_hbm, out_ref,
    blocks, weights, mine, sent, got, gate_rows,
    load_sem, weight_sem, x_send, x_recv, up_send, down_send, y_send, core_send, unit_recv,
    part_send, part_recv,
):
    tokens, width = rows_ref.shape
    half = width // 2
    held = weights_hbm.shape[0]
    chunk = FF // CHUNKS
    c = lax.axis_index("ctx")
    e = lax.axis_index("ep")
    z, y, k = e // 4, (e // 2) % 2, e % 2
    chip = 2 * z + y
    x_peer = {"ctx": 1 - c, "ep": e}
    y_peer = {"ctx": c, "ep": 4 * z + 2 * (1 - y) + k}
    core_peer = {"ctx": c, "ep": 4 * z + 2 * y + 1 - k}
    up_peer = {"ctx": c, "ep": e + 4}
    down_peer = {"ctx": c, "ep": e - 4}
    not_top, not_bottom = z < ZS - 1, z > 0

    barrier = pltpu.get_barrier_semaphore()

    def greet(peer):
        pl.semaphore_signal(barrier, inc=1, device_id=peer, device_id_type=pl.DeviceIdType.MESH)

    greet(x_peer)
    greet(y_peer)
    greet(core_peer)

    @pl.when(not_top)
    def _():
        greet(up_peer)

    @pl.when(not_bottom)
    def _():
        greet(down_peer)

    load = pltpu.make_async_copy(
        rows_ref.at[:, pl.ds(pl.multiple_of(c * half, half), half)],
        blocks.at[chip, k, c, pl.ds(0, tokens)],
        load_sem,
    )
    load.start()
    weight_loads = [
        pltpu.make_async_copy(weights_hbm.at[j], weights.at[j], weight_sem.at[j]) for j in range(held)
    ]

    expert = lax.broadcasted_iota(jnp.int32, (32, tokens), 0)
    ids = ids_ref[...]
    gates = gates_ref[...].astype(jnp.float32)
    marks = jnp.zeros((32, tokens), jnp.float32)
    gate_of = jnp.zeros((32, tokens), jnp.float32)
    for t in range(TOP):
        same = ids[t : t + 1] == expert
        marks = marks + jnp.where(same, 1.0, 0.0)
        gate_of = gate_of + jnp.where(same, gates[t : t + 1], 0.0)
    earlier = (
        lax.broadcasted_iota(jnp.int32, (tokens, tokens), 0)
        < lax.broadcasted_iota(jnp.int32, (tokens, tokens), 1)
    )
    rank = jnp.dot(
        marks.astype(jnp.bfloat16),
        jnp.where(earlier, 1.0, 0.0).astype(jnp.bfloat16),
        preferred_element_type=jnp.float32,
    )
    slots = jnp.where(marks > 0, rank, -1.0)
    table = jnp.concatenate(
        [slots[:16], slots[16:], gate_of[:16], gate_of[16:], jnp.zeros((META, half - 512), jnp.float32)],
        axis=1,
    )
    blocks[chip, k, c, tokens:, :] = table.astype(jnp.bfloat16)
    blocks[chip, k, 1 - c, tokens:, 512:] = jnp.zeros((META, half - 512), jnp.bfloat16)

    pl.semaphore_wait(barrier, 3 + (z + ZS - 1) // ZS + (2 * ZS - 2 - z) // ZS)

    def remote(src, dst, send_sem, recv_sem, peer):
        return pltpu.make_async_remote_copy(
            src_ref=src, dst_ref=dst, send_sem=send_sem, recv_sem=recv_sem,
            device_id=peer, device_id_type=pl.DeviceIdType.MESH,
        )

    def x_rows(plane):
        return remote(
            rows_ref.at[:, pl.ds(pl.multiple_of((1 - c) * half, half), half)],
            blocks.at[chip, k, plane, pl.ds(0, tokens)],
            x_send.at[0], x_recv.at[0], x_peer,
        )

    def x_table(plane):
        return remote(
            blocks.at[chip, k, plane, pl.ds(tokens, META), pl.ds(0, 512)],
            blocks.at[chip, k, plane, pl.ds(tokens, META), pl.ds(0, 512)],
            x_send.at[1], x_recv.at[1], x_peer,
        )

    x_rows(c).start()
    x_table(c).start()
    for w in weight_loads:
        w.start()
    load.wait()

    def unit_copy(g, core, plane, send_sem, peer):
        unit = blocks.at[g, core, plane]
        return remote(unit, unit, send_sem, unit_recv.at[(g * 2 + core) * 2 + plane], peer)

    def each_send(step, plane, act):
        zs, ys, other = chip_at_step(step, z, y)
        g = 2 * zs + ys

        act(unit_copy(g, k, plane, core_send.at[g * 2 + plane], core_peer))

        @pl.when((other == 0) & not_top & (zs <= z))
        def _():
            act(unit_copy(g, k, plane, up_send.at[zs * 2 + plane], up_peer))

        @pl.when((other == 0) & not_bottom & (zs >= z))
        def _():
            act(unit_copy(g, k, plane, down_send.at[zs * 2 + plane], down_peer))

        @pl.when(other == 0)
        def _():
            act(unit_copy(g, k, plane, y_send.at[zs * 2 + plane], y_peer))

    def part_copy(g, n):
        at = g * CHUNKS + n
        return remote(sent.at[g, n], got.at[g, n], part_send.at[at], part_recv.at[at], x_peer)

    def place(g, plane, gates_too):
        x = jnp.concatenate([blocks[g, core, plane, :tokens, :] for core in range(2)], axis=0)
        pick = lax.broadcasted_iota(jnp.int32, (META, 128), 0)
        row = lax.broadcasted_iota(jnp.int32, (2 * cap, 2 * tokens), 0).astype(jnp.float32)

        def lines(first, j):
            at = pl.multiple_of((e // 8) * 128 + first, 128)
            return [
                jnp.sum(
                    jnp.where(
                        pick == (e % 8) * 2 + j,
                        blocks[g, core, plane, tokens:, pl.ds(at, 128)].astype(jnp.float32),
                        0.0,
                    ),
                    axis=0,
                    keepdims=True,
                )
                for core in range(2)
            ]

        hots, gate_columns = [], []
        for j in range(held):
            near, far = lines(0, j)
            far = jnp.where(far >= 0, far + float(cap), -1.0)
            hot = row == jnp.concatenate([near, far], axis=1)
            hots.append(jnp.where(hot, 1.0, 0.0))
            if gates_too:
                gate_line = jnp.concatenate(lines(256, j), axis=1)
                gate_columns.append(jnp.sum(jnp.where(hot, gate_line, 0.0), axis=1, keepdims=True))
        if gates_too:
            column = jnp.concatenate(gate_columns, axis=0)
            gate_rows[g] = jnp.broadcast_to(column, (held * 2 * cap, 128))
        return jnp.dot(
            jnp.concatenate(hots, axis=0).astype(jnp.bfloat16), x, preferred_element_type=jnp.float32
        )

    def compute(g, theirs, ours):
        rows = [slice(j * 2 * cap, (j + 1) * 2 * cap) for j in range(held)]
        chosen = [
            jnp.concatenate([theirs[r], ours[r]], axis=0).astype(jnp.bfloat16) for r in rows
        ]
        for n in range(CHUNKS):
            for side in range(2):
                columns = slice(side * FF + n * chunk, side * FF + (n + 1) * chunk)
                here = slice(side * chunk, (side + 1) * chunk)
                parts = [
                    jnp.dot(chosen[j], weights[j, :, columns], preferred_element_type=jnp.float32)
                    for j in range(held)
                ]
                sent[g, n, :, here] = encode(
                    jnp.concatenate([p[: 2 * cap] for p in parts], axis=0), scale
                )
                mine[g, n, :, here] = jnp.concatenate([p[2 * cap :] for p in parts], axis=0)
            part_copy(g, n).start()

    def work(step, carry):
        zs, ys, other = chip_at_step(step, z, y)
        g = 2 * zs + ys

        @pl.when(step > 0)
        def _():
            unit_copy(g, k, c, core_send.at[g * 2 + c], core_peer).wait_recv()

        each_send(step, c, lambda copy: copy.start())
        unit_copy(g, 1 - k, c, core_send.at[g * 2 + c], core_peer).wait_recv()
        ours = place(g, c, True)

        @pl.when(step == 0)
        def _():
            for w in weight_loads:
                w.wait()
            x_rows(1 - c).wait_recv()
            x_table(1 - c).wait_recv()

        @pl.when(step > 0)
        def _():
            unit_copy(g, k, 1 - c, core_send.at[g * 2 + 1 - c], core_peer).wait_recv()

        each_send(step, 1 - c, lambda copy: copy.start())
        unit_copy(g, 1 - k, 1 - c, core_send.at[g * 2 + 1 - c], core_peer).wait_recv()
        compute(g, place(g, 1 - c, False), ours)
        return carry

    lax.fori_loop(0, CHIPS, work, 0)

    def finish(step, carry):
        zs, ys, _ = chip_at_step(step, z, y)
        g = 2 * zs + ys
        gate_column = gate_rows[g, :, 0:1]
        for plane in (c, 1 - c):
            each_send(step, plane, lambda copy: copy.wait_send())
        for n in range(CHUNKS):
            part_copy(g, n).wait_recv()
            first = mine[g, n, :, :chunk] + decode(got[g, n, :, :chunk], scale)
            second = mine[g, n, :, chunk:] + decode(got[g, n, :, chunk:], scale)
            hidden = first / (1.0 + jnp.exp(-first)) * second * gate_column
            for j in range(held):
                for core in range(2):
                    low = (j * 2 + core) * cap
                    out_ref[0, j, 2 * g + core, :, n * chunk : (n + 1) * chunk] = hidden[
                        low : low + cap
                    ].astype(jnp.bfloat16)
            part_copy(g, n).wait_send()
        return carry

    x_rows(c).wait_send()
    x_table(c).wait_send()
    lax.fori_loop(0, CHIPS, finish, 0)


def kernel_shards(moe_rows, expert_ids, expert_gates, expert_weights):
    sources = lax.axis_size("ep")
    tokens, width = moe_rows.shape
    held, half, columns = expert_weights.shape
    cap = max(2, 9 * tokens * TOP // (8 * sources * held))
    part_rows = held * 2 * cap
    scale = 2.0 ** math.floor(math.log2(49152.0 / (half * ROW_BOUND * WEIGHT_BOUND)))
    dma = pltpu.SemaphoreType.DMA
    vmem = pl.BlockSpec(memory_space=pltpu.VMEM)
    hbm = pl.BlockSpec(memory_space=pl.ANY)
    return pl.pallas_call(
        functools.partial(kernel, cap, scale),
        out_shape=pltpu.VMEM((1, held, sources, cap, columns // 2), jnp.bfloat16),
        in_specs=[hbm, vmem, vmem, hbm],
        out_specs=vmem,
        scratch_shapes=[
            pltpu.VMEM((CHIPS, 2, 2, tokens + META, half), jnp.bfloat16),
            pltpu.VMEM((held, half, columns), jnp.bfloat16),
            pltpu.VMEM((CHIPS, CHUNKS, part_rows, columns // CHUNKS), jnp.float32),
            pltpu.VMEM((CHIPS, CHUNKS, part_rows, columns // CHUNKS), jnp.bfloat16),
            pltpu.VMEM((CHIPS, CHUNKS, part_rows, columns // CHUNKS), jnp.bfloat16),
            pltpu.VMEM((CHIPS, part_rows, 128), jnp.float32),
            dma,
            dma((held,)),
            dma((2,)),
            dma((2,)),
            dma((2 * ZS,)),
            dma((2 * ZS,)),
            dma((2 * ZS,)),
            dma((2 * CHIPS,)),
            dma((4 * CHIPS,)),
            dma((CHIPS * CHUNKS,)),
            dma((CHIPS * CHUNKS,)),
        ],
        compiler_params=pltpu.CompilerParams(
            collective_id=0, has_side_effects=True, vmem_limit_bytes=56 * 1024 * 1024
        ),
        cost_estimate=pl.CostEstimate(
            flops=2 * CHIPS * held * 4 * cap * half * columns,
            bytes_accessed=held * half * columns * 2,
            transcendentals=0,
        ),
    )(moe_rows, expert_ids.T, expert_gates.T, expert_weights)


def solution(mesh):
    in_specs = (
        P(("ctx", "ep"), None),
        P(("ctx", "ep"), None),
        P(("ctx", "ep"), None),
        P("ep", "ctx", None),
    )
    out_specs = P("ctx", "ep", None, None, None)
    fits = mesh.shape["ctx"] == 2 and mesh.shape["ep"] == 2 * CHIPS
    body = kernel_shards if fits else general_shards
    return jax.shard_map(body, mesh=mesh, in_specs=in_specs, out_specs=out_specs, check_vma=False)
```

```python
import functools
import math

import jax
import jax.numpy as jnp
from jax import lax
from jax.experimental import pallas as pl
from jax.experimental.pallas import tpu as pltpu
from jax.sharding import PartitionSpec as P

FF = 768
TOP = 8
ROW_BOUND = 6.0
WEIGHT_BOUND = 0.125
META = 16
ZS = 4
CHIPS = 8
CHUNKS = 3


def place_rows(block_rows, block_ids, block_gates, experts, capacity):
    flat_ids = block_ids.reshape(-1)
    markers = (flat_ids[:, None] == jnp.arange(experts, dtype=jnp.int32)[None, :]).astype(jnp.int32)
    ranking = jnp.cumsum(markers, axis=0) - markers
    slot_index = jnp.sum(ranking * markers, axis=1)
    places = flat_ids * capacity + slot_index
    owners = jnp.arange(flat_ids.shape[0], dtype=jnp.int32) // block_ids.shape[1]
    buffer = (
        jnp.zeros((experts * capacity, block_rows.shape[1]), block_rows.dtype)
        .at[places]
        .set(block_rows[owners])
    )
    gate_buffer = (
        jnp.zeros((experts * capacity,), block_gates.dtype).at[places].set(block_gates.reshape(-1))
    )
    return (
        buffer.reshape(experts, capacity, block_rows.shape[1]),
        gate_buffer.reshape(experts, capacity),
    )


def project(inputs, weights):
    return jnp.einsum("sucd,udf->uscf", inputs, weights, preferred_element_type=jnp.float32)


def activate(before, gate_values):
    scaled = jnp.transpose(gate_values, (1, 0, 2)).astype(jnp.float32)[..., None]
    return (jax.nn.silu(before[..., :FF]) * before[..., FF:] * scaled).astype(jnp.bfloat16)


def general_shards(moe_rows, expert_ids, expert_gates, expert_weights):
    sources = lax.axis_size("ep")
    held_experts = expert_weights.shape[0]
    experts = sources * held_experts
    row_count = moe_rows.shape[0]
    capacity = max(2, 9 * row_count * TOP // (8 * experts))
    buffer, gate_buffer = place_rows(moe_rows, expert_ids, expert_gates, experts, capacity)
    buffer = buffer.reshape(sources, held_experts, capacity, buffer.shape[2])
    gate_buffer = gate_buffer.reshape(sources, held_experts, capacity)
    arrived, arrived_gates = (
        lax.all_to_all(buffer, "ep", split_axis=0, concat_axis=0, tiled=True),
        lax.all_to_all(gate_buffer, "ep", split_axis=0, concat_axis=0, tiled=True),
    )
    before = project(arrived, lax.all_gather(expert_weights, "ctx", axis=1, tiled=True))
    hidden = activate(before, arrived_gates)
    return hidden[None]


def chip_at_step(step, z, y):
    first, last, odd = (7 - step) // 7, step // 7, step % 2
    other = (1 - odd) * (1 - first) + last
    i = odd * ((step + 1) // 2) + (1 - odd) * (step // 2 - 1) + first - last
    mirror = z // 2
    inner = mirror * (ZS - 1 - z) + (1 - mirror) * z
    near = 1 - i // 2
    w = inner * (near * (1 - i) + (1 - near) * i) + (1 - inner) * i
    zs = mirror * (ZS - 1 - w) + (1 - mirror) * w
    ys = y + other * (1 - 2 * y)
    return zs, ys, other


def encode(p, scale):
    q = p * scale
    q2 = q * q
    q4 = q2 * q2
    q8 = q4 * q4
    return jnp.where(q < 0, -q8, q8).astype(jnp.bfloat16)


def decode(code, scale):
    v = code.astype(jnp.float32)
    size = jnp.exp(jnp.log(jnp.abs(v)) * 0.125) * (1.0 / scale)
    return jnp.where(v < 0, -size, size)


def kernel(
    cap, scale,
    rows_ref, ids_ref, gates_ref, weights_hbm, out_ref,
    blocks, weights, mine, sent, got, gate_rows,
    load_sem, weight_sem, x_send, x_recv, up_send, down_send, y_send, core_send, unit_recv,
    part_send, part_recv,
):
    tokens, width = rows_ref.shape
    half = width // 2
    held = weights_hbm.shape[0]
    chunk = FF // CHUNKS
    c = lax.axis_index("ctx")
    e = lax.axis_index("ep")
    z, y, k = e // 4, (e // 2) % 2, e % 2
    chip = 2 * z + y
    x_peer = {"ctx": 1 - c, "ep": e}
    y_peer = {"ctx": c, "ep": 4 * z + 2 * (1 - y) + k}
    core_peer = {"ctx": c, "ep": 4 * z + 2 * y + 1 - k}
    up_peer = {"ctx": c, "ep": e + 4}
    down_peer = {"ctx": c, "ep": e - 4}
    not_top, not_bottom = z < ZS - 1, z > 0

    barrier = pltpu.get_barrier_semaphore()

    def greet(peer):
        pl.semaphore_signal(barrier, inc=1, device_id=peer, device_id_type=pl.DeviceIdType.MESH)

    greet(x_peer)
    greet(y_peer)
    greet(core_peer)

    @pl.when(not_top)
    def _():
        greet(up_peer)

    @pl.when(not_bottom)
    def _():
        greet(down_peer)

    load = pltpu.make_async_copy(
        rows_ref.at[:, pl.ds(pl.multiple_of(c * half, half), half)],
        blocks.at[chip, k, c, pl.ds(0, tokens)],
        load_sem,
    )
    load.start()
    weight_loads = [
        pltpu.make_async_copy(weights_hbm.at[j], weights.at[j], weight_sem.at[j]) for j in range(held)
    ]

    expert = lax.broadcasted_iota(jnp.int32, (32, tokens), 0)
    ids = ids_ref[...]
    gates = gates_ref[...].astype(jnp.float32)
    marks = jnp.zeros((32, tokens), jnp.float32)
    gate_of = jnp.zeros((32, tokens), jnp.float32)
    for t in range(TOP):
        same = ids[t : t + 1] == expert
        marks = marks + jnp.where(same, 1.0, 0.0)
        gate_of = gate_of + jnp.where(same, gates[t : t + 1], 0.0)
    earlier = (
        lax.broadcasted_iota(jnp.int32, (tokens, tokens), 0)
        < lax.broadcasted_iota(jnp.int32, (tokens, tokens), 1)
    )
    rank = jnp.dot(
        marks.astype(jnp.bfloat16),
        jnp.where(earlier, 1.0, 0.0).astype(jnp.bfloat16),
        preferred_element_type=jnp.float32,
    )
    slots = jnp.where(marks > 0, rank, -1.0)
    table = jnp.concatenate(
        [slots[:16], slots[16:], gate_of[:16], gate_of[16:], jnp.zeros((META, half - 512), jnp.float32)],
        axis=1,
    )
    blocks[chip, k, c, tokens:, :] = table.astype(jnp.bfloat16)
    blocks[chip, k, 1 - c, tokens:, 512:] = jnp.zeros((META, half - 512), jnp.bfloat16)

    pl.semaphore_wait(barrier, 3 + (z + ZS - 1) // ZS + (2 * ZS - 2 - z) // ZS)

    def remote(src, dst, send_sem, recv_sem, peer):
        return pltpu.make_async_remote_copy(
            src_ref=src, dst_ref=dst, send_sem=send_sem, recv_sem=recv_sem,
            device_id=peer, device_id_type=pl.DeviceIdType.MESH,
        )

    def x_rows(plane):
        return remote(
            rows_ref.at[:, pl.ds(pl.multiple_of((1 - c) * half, half), half)],
            blocks.at[chip, k, plane, pl.ds(0, tokens)],
            x_send.at[0], x_recv.at[0], x_peer,
        )

    def x_table(plane):
        return remote(
            blocks.at[chip, k, plane, pl.ds(tokens, META), pl.ds(0, 512)],
            blocks.at[chip, k, plane, pl.ds(tokens, META), pl.ds(0, 512)],
            x_send.at[1], x_recv.at[1], x_peer,
        )

    x_rows(c).start()
    x_table(c).start()
    for w in weight_loads:
        w.start()
    load.wait()

    def unit_copy(g, core, plane, send_sem, peer):
        unit = blocks.at[g, core, plane]
        return remote(unit, unit, send_sem, unit_recv.at[(g * 2 + core) * 2 + plane], peer)

    def each_send(step, plane, act):
        zs, ys, other = chip_at_step(step, z, y)
        g = 2 * zs + ys

        act(unit_copy(g, k, plane, core_send.at[g * 2 + plane], core_peer))

        @pl.when((other == 0) & not_top & (zs <= z))
        def _():
            act(unit_copy(g, k, plane, up_send.at[zs * 2 + plane], up_peer))

        @pl.when((other == 0) & not_bottom & (zs >= z))
        def _():
            act(unit_copy(g, k, plane, down_send.at[zs * 2 + plane], down_peer))

        @pl.when(other == 0)
        def _():
            act(unit_copy(g, k, plane, y_send.at[zs * 2 + plane], y_peer))

    def part_copy(g, n):
        at = g * CHUNKS + n
        return remote(sent.at[g, n], got.at[g, n], part_send.at[at], part_recv.at[at], x_peer)

    def place(g, plane, gates_too):
        x = jnp.concatenate([blocks[g, core, plane, :tokens, :] for core in range(2)], axis=0)
        pick = lax.broadcasted_iota(jnp.int32, (META, 128), 0)
        row = lax.broadcasted_iota(jnp.int32, (2 * cap, 2 * tokens), 0).astype(jnp.float32)

        def lines(first, j):
            at = pl.multiple_of((e // 8) * 128 + first, 128)
            return [
                jnp.sum(
                    jnp.where(
                        pick == (e % 8) * 2 + j,
                        blocks[g, core, plane, tokens:, pl.ds(at, 128)].astype(jnp.float32),
                        0.0,
                    ),
                    axis=0,
                    keepdims=True,
                )
                for core in range(2)
            ]

        hots, gate_columns = [], []
        for j in range(held):
            near, far = lines(0, j)
            far = jnp.where(far >= 0, far + float(cap), -1.0)
            hot = row == jnp.concatenate([near, far], axis=1)
            hots.append(jnp.where(hot, 1.0, 0.0))
            if gates_too:
                gate_line = jnp.concatenate(lines(256, j), axis=1)
                gate_columns.append(jnp.sum(jnp.where(hot, gate_line, 0.0), axis=1, keepdims=True))
        if gates_too:
            column = jnp.concatenate(gate_columns, axis=0)
            gate_rows[g] = jnp.broadcast_to(column, (held * 2 * cap, 128))
        return jnp.dot(
            jnp.concatenate(hots, axis=0).astype(jnp.bfloat16), x, preferred_element_type=jnp.float32
        )

    def compute(g, theirs, ours):
        rows = [slice(j * 2 * cap, (j + 1) * 2 * cap) for j in range(held)]
        chosen = [
            jnp.concatenate([theirs[r], ours[r]], axis=0).astype(jnp.bfloat16) for r in rows
        ]
        for n in range(CHUNKS):
            for side in range(2):
                columns = slice(side * FF + n * chunk, side * FF + (n + 1) * chunk)
                here = slice(side * chunk, (side + 1) * chunk)
                parts = [
                    jnp.dot(chosen[j], weights[j, :, columns], preferred_element_type=jnp.float32)
                    for j in range(held)
                ]
                sent[g, n, :, here] = encode(
                    jnp.concatenate([p[: 2 * cap] for p in parts], axis=0), scale
                )
                mine[g, n, :, here] = jnp.concatenate([p[2 * cap :] for p in parts], axis=0)
            part_copy(g, n).start()

    def chip_of(step):
        zs, ys, _ = chip_at_step(step, z, y)
        return 2 * zs + ys

    def from_core(g, plane):
        unit_copy(g, 1 - k, plane, core_send.at[g * 2 + plane], core_peer).wait_recv()

    def forward(step):
        g = chip_of(step)
        for plane in (c, 1 - c):
            unit_copy(g, k, plane, core_send.at[g * 2 + plane], core_peer).wait_recv()
            each_send(step, plane, lambda copy: copy.start())

    def work(step, carry):
        @pl.when(step % 2 == 1)
        def _():
            forward(step)

            @pl.when(step < CHIPS - 1)
            def _():
                forward(step + 1)

        g = chip_of(step)
        from_core(g, c)
        from_core(g, 1 - c)
        ours = place(g, c, True)
        compute(g, place(g, 1 - c, False), ours)
        return carry

    each_send(0, c, lambda copy: copy.start())
    from_core(chip, c)
    ours = place(chip, c, True)
    for w in weight_loads:
        w.wait()
    x_rows(1 - c).wait_recv()
    x_table(1 - c).wait_recv()
    each_send(0, 1 - c, lambda copy: copy.start())
    from_core(chip, 1 - c)
    compute(chip, place(chip, 1 - c, False), ours)
    lax.fori_loop(1, CHIPS, work, 0)

    def finish(step, carry):
        zs, ys, _ = chip_at_step(step, z, y)
        g = 2 * zs + ys
        gate_column = gate_rows[g, :, 0:1]
        for plane in (c, 1 - c):
            each_send(step, plane, lambda copy: copy.wait_send())
        for n in range(CHUNKS):
            part_copy(g, n).wait_recv()
            first = mine[g, n, :, :chunk] + decode(got[g, n, :, :chunk], scale)
            second = mine[g, n, :, chunk:] + decode(got[g, n, :, chunk:], scale)
            hidden = first / (1.0 + jnp.exp(-first)) * second * gate_column
            for j in range(held):
                for core in range(2):
                    low = (j * 2 + core) * cap
                    out_ref[0, j, 2 * g + core, :, n * chunk : (n + 1) * chunk] = hidden[
                        low : low + cap
                    ].astype(jnp.bfloat16)
            part_copy(g, n).wait_send()
        return carry

    x_rows(c).wait_send()
    x_table(c).wait_send()
    lax.fori_loop(0, CHIPS, finish, 0)


def kernel_shards(moe_rows, expert_ids, expert_gates, expert_weights):
    sources = lax.axis_size("ep")
    tokens, width = moe_rows.shape
    held, half, columns = expert_weights.shape
    cap = max(2, 9 * tokens * TOP // (8 * sources * held))
    part_rows = held * 2 * cap
    scale = 2.0 ** math.floor(math.log2(49152.0 / (half * ROW_BOUND * WEIGHT_BOUND)))
    dma = pltpu.SemaphoreType.DMA
    vmem = pl.BlockSpec(memory_space=pltpu.VMEM)
    hbm = pl.BlockSpec(memory_space=pl.ANY)
    return pl.pallas_call(
        functools.partial(kernel, cap, scale),
        out_shape=pltpu.VMEM((1, held, sources, cap, columns // 2), jnp.bfloat16),
        in_specs=[hbm, vmem, vmem, hbm],
        out_specs=vmem,
        scratch_shapes=[
            pltpu.VMEM((CHIPS, 2, 2, tokens + META, half), jnp.bfloat16),
            pltpu.VMEM((held, half, columns), jnp.bfloat16),
            pltpu.VMEM((CHIPS, CHUNKS, part_rows, columns // CHUNKS), jnp.float32),
            pltpu.VMEM((CHIPS, CHUNKS, part_rows, columns // CHUNKS), jnp.bfloat16),
            pltpu.VMEM((CHIPS, CHUNKS, part_rows, columns // CHUNKS), jnp.bfloat16),
            pltpu.VMEM((CHIPS, part_rows, 128), jnp.float32),
            dma,
            dma((held,)),
            dma((2,)),
            dma((2,)),
            dma((2 * ZS,)),
            dma((2 * ZS,)),
            dma((2 * ZS,)),
            dma((2 * CHIPS,)),
            dma((4 * CHIPS,)),
            dma((CHIPS * CHUNKS,)),
            dma((CHIPS * CHUNKS,)),
        ],
        compiler_params=pltpu.CompilerParams(
            collective_id=0, has_side_effects=True, vmem_limit_bytes=56 * 1024 * 1024
        ),
        cost_estimate=pl.CostEstimate(
            flops=2 * CHIPS * held * 4 * cap * half * columns,
            bytes_accessed=held * half * columns * 2,
            transcendentals=0,
        ),
    )(moe_rows, expert_ids.T, expert_gates.T, expert_weights)


def solution(mesh):
    in_specs = (
        P(("ctx", "ep"), None),
        P(("ctx", "ep"), None),
        P(("ctx", "ep"), None),
        P("ep", "ctx", None),
    )
    out_specs = P("ctx", "ep", None, None, None)
    fits = mesh.shape["ctx"] == 2 and mesh.shape["ep"] == 2 * CHIPS
    body = kernel_shards if fits else general_shards
    return jax.shard_map(body, mesh=mesh, in_specs=in_specs, out_specs=out_specs, check_vma=False)
```

```python
import functools
import math

import jax
import jax.numpy as jnp
from jax import lax
from jax.experimental import pallas as pl
from jax.experimental.pallas import tpu as pltpu
from jax.sharding import PartitionSpec as P

FF = 768
TOP = 8
ROW_BOUND = 6.0
WEIGHT_BOUND = 0.125
META = 16
ZS = 4
CHIPS = 8
CHUNKS = 3


def place_rows(block_rows, block_ids, block_gates, experts, capacity):
    flat_ids = block_ids.reshape(-1)
    markers = (flat_ids[:, None] == jnp.arange(experts, dtype=jnp.int32)[None, :]).astype(jnp.int32)
    ranking = jnp.cumsum(markers, axis=0) - markers
    slot_index = jnp.sum(ranking * markers, axis=1)
    places = flat_ids * capacity + slot_index
    owners = jnp.arange(flat_ids.shape[0], dtype=jnp.int32) // block_ids.shape[1]
    buffer = (
        jnp.zeros((experts * capacity, block_rows.shape[1]), block_rows.dtype)
        .at[places]
        .set(block_rows[owners])
    )
    gate_buffer = (
        jnp.zeros((experts * capacity,), block_gates.dtype).at[places].set(block_gates.reshape(-1))
    )
    return (
        buffer.reshape(experts, capacity, block_rows.shape[1]),
        gate_buffer.reshape(experts, capacity),
    )


def project(inputs, weights):
    return jnp.einsum("sucd,udf->uscf", inputs, weights, preferred_element_type=jnp.float32)


def activate(before, gate_values):
    scaled = jnp.transpose(gate_values, (1, 0, 2)).astype(jnp.float32)[..., None]
    return (jax.nn.silu(before[..., :FF]) * before[..., FF:] * scaled).astype(jnp.bfloat16)


def general_shards(moe_rows, expert_ids, expert_gates, expert_weights):
    sources = lax.axis_size("ep")
    held_experts = expert_weights.shape[0]
    experts = sources * held_experts
    row_count = moe_rows.shape[0]
    capacity = max(2, 9 * row_count * TOP // (8 * experts))
    buffer, gate_buffer = place_rows(moe_rows, expert_ids, expert_gates, experts, capacity)
    buffer = buffer.reshape(sources, held_experts, capacity, buffer.shape[2])
    gate_buffer = gate_buffer.reshape(sources, held_experts, capacity)
    arrived, arrived_gates = (
        lax.all_to_all(buffer, "ep", split_axis=0, concat_axis=0, tiled=True),
        lax.all_to_all(gate_buffer, "ep", split_axis=0, concat_axis=0, tiled=True),
    )
    before = project(arrived, lax.all_gather(expert_weights, "ctx", axis=1, tiled=True))
    hidden = activate(before, arrived_gates)
    return hidden[None]


def chip_at_step(step, z, y):
    first, last, odd = (7 - step) // 7, step // 7, step % 2
    other = (1 - odd) * (1 - first) + last
    i = odd * ((step + 1) // 2) + (1 - odd) * (step // 2 - 1) + first - last
    mirror = z // 2
    inner = mirror * (ZS - 1 - z) + (1 - mirror) * z
    near = 1 - i // 2
    w = inner * (near * (1 - i) + (1 - near) * i) + (1 - inner) * i
    zs = mirror * (ZS - 1 - w) + (1 - mirror) * w
    ys = y + other * (1 - 2 * y)
    return zs, ys, other


def encode(p, scale):
    q = p * scale
    q2 = q * q
    q4 = q2 * q2
    q8 = q4 * q4
    return jnp.where(q < 0, -q8, q8).astype(jnp.bfloat16)


def decode(code, scale):
    v = code.astype(jnp.float32)
    size = jnp.exp(jnp.log(jnp.abs(v)) * 0.125) * (1.0 / scale)
    return jnp.where(v < 0, -size, size)


def kernel(
    cap, scale,
    rows_ref, ids_hbm, gates_hbm, weights_hbm, out_ref,
    blocks, weights, mine, sent, got, gate_rows,
    ids_ref, gates_ref, load_sem, small_sem, weight_sem, x_send, x_recv, up_send, down_send, y_send, core_send, unit_recv,
    part_send, part_recv,
):
    tokens, width = rows_ref.shape
    half = width // 2
    held = weights_hbm.shape[0]
    chunk = FF // CHUNKS
    c = lax.axis_index("ctx")
    e = lax.axis_index("ep")
    z, y, k = e // 4, (e // 2) % 2, e % 2
    chip = 2 * z + y
    x_peer = {"ctx": 1 - c, "ep": e}
    y_peer = {"ctx": c, "ep": 4 * z + 2 * (1 - y) + k}
    core_peer = {"ctx": c, "ep": 4 * z + 2 * y + 1 - k}
    up_peer = {"ctx": c, "ep": e + 4}
    down_peer = {"ctx": c, "ep": e - 4}
    not_top, not_bottom = z < ZS - 1, z > 0

    barrier = pltpu.get_barrier_semaphore()

    def greet(peer):
        pl.semaphore_signal(barrier, inc=1, device_id=peer, device_id_type=pl.DeviceIdType.MESH)

    greet(x_peer)
    greet(y_peer)
    greet(core_peer)

    @pl.when(not_top)
    def _():
        greet(up_peer)

    @pl.when(not_bottom)
    def _():
        greet(down_peer)

    load = pltpu.make_async_copy(
        rows_ref.at[:, pl.ds(pl.multiple_of(c * half, half), half)],
        blocks.at[chip, k, c, pl.ds(0, tokens)],
        load_sem,
    )
    small_loads = [
        pltpu.make_async_copy(ids_hbm, ids_ref, small_sem.at[0]),
        pltpu.make_async_copy(gates_hbm, gates_ref, small_sem.at[1]),
    ]
    for copy in small_loads:
        copy.start()
    load.start()
    weight_loads = [
        pltpu.make_async_copy(weights_hbm.at[j], weights.at[j], weight_sem.at[j]) for j in range(held)
    ]

    pl.semaphore_wait(barrier, 3 + (z + ZS - 1) // ZS + (2 * ZS - 2 - z) // ZS)

    def remote(src, dst, send_sem, recv_sem, peer):
        return pltpu.make_async_remote_copy(
            src_ref=src, dst_ref=dst, send_sem=send_sem, recv_sem=recv_sem,
            device_id=peer, device_id_type=pl.DeviceIdType.MESH,
        )

    def x_rows(plane):
        return remote(
            rows_ref.at[:, pl.ds(pl.multiple_of((1 - c) * half, half), half)],
            blocks.at[chip, k, plane, pl.ds(0, tokens)],
            x_send.at[0], x_recv.at[0], x_peer,
        )

    def x_table(plane):
        return remote(
            blocks.at[chip, k, plane, pl.ds(tokens, META), pl.ds(0, 512)],
            blocks.at[chip, k, plane, pl.ds(tokens, META), pl.ds(0, 512)],
            x_send.at[1], x_recv.at[1], x_peer,
        )

    x_rows(c).start()
    for copy in small_loads:
        copy.wait()

    expert = lax.broadcasted_iota(jnp.int32, (32, tokens), 0)
    ids = ids_ref[...]
    gates = gates_ref[...].astype(jnp.float32)
    marks = jnp.zeros((32, tokens), jnp.float32)
    gate_of = jnp.zeros((32, tokens), jnp.float32)
    for t in range(TOP):
        same = ids[t : t + 1] == expert
        marks = marks + jnp.where(same, 1.0, 0.0)
        gate_of = gate_of + jnp.where(same, gates[t : t + 1], 0.0)
    earlier = (
        lax.broadcasted_iota(jnp.int32, (tokens, tokens), 0)
        < lax.broadcasted_iota(jnp.int32, (tokens, tokens), 1)
    )
    rank = jnp.dot(
        marks.astype(jnp.bfloat16),
        jnp.where(earlier, 1.0, 0.0).astype(jnp.bfloat16),
        preferred_element_type=jnp.float32,
    )
    slots = jnp.where(marks > 0, rank, -1.0)
    table = jnp.concatenate(
        [slots[:16], slots[16:], gate_of[:16], gate_of[16:], jnp.zeros((META, half - 512), jnp.float32)],
        axis=1,
    )
    blocks[chip, k, c, tokens:, :] = table.astype(jnp.bfloat16)
    blocks[chip, k, 1 - c, tokens:, 512:] = jnp.zeros((META, half - 512), jnp.bfloat16)

    x_table(c).start()
    for w in weight_loads:
        w.start()
    load.wait()

    def unit_copy(g, core, plane, send_sem, peer):
        unit = blocks.at[g, core, plane]
        return remote(unit, unit, send_sem, unit_recv.at[(g * 2 + core) * 2 + plane], peer)

    def each_send(step, plane, act):
        zs, ys, other = chip_at_step(step, z, y)
        g = 2 * zs + ys

        act(unit_copy(g, k, plane, core_send.at[g * 2 + plane], core_peer))

        @pl.when((other == 0) & not_top & (zs <= z))
        def _():
            act(unit_copy(g, k, plane, up_send.at[zs * 2 + plane], up_peer))

        @pl.when((other == 0) & not_bottom & (zs >= z))
        def _():
            act(unit_copy(g, k, plane, down_send.at[zs * 2 + plane], down_peer))

        @pl.when(other == 0)
        def _():
            act(unit_copy(g, k, plane, y_send.at[zs * 2 + plane], y_peer))

    def part_copy(g, n):
        at = g * CHUNKS + n
        return remote(sent.at[g, n], got.at[g, n], part_send.at[at], part_recv.at[at], x_peer)

    def place(g, plane, gates_too):
        x = jnp.concatenate([blocks[g, core, plane, :tokens, :] for core in range(2)], axis=0)
        pick = lax.broadcasted_iota(jnp.int32, (META, 128), 0)
        row = lax.broadcasted_iota(jnp.int32, (2 * cap, 2 * tokens), 0).astype(jnp.float32)

        def lines(first, j):
            at = pl.multiple_of((e // 8) * 128 + first, 128)
            return [
                jnp.sum(
                    jnp.where(
                        pick == (e % 8) * 2 + j,
                        blocks[g, core, plane, tokens:, pl.ds(at, 128)].astype(jnp.float32),
                        0.0,
                    ),
                    axis=0,
                    keepdims=True,
                )
                for core in range(2)
            ]

        hots, gate_columns = [], []
        for j in range(held):
            near, far = lines(0, j)
            far = jnp.where(far >= 0, far + float(cap), -1.0)
            hot = row == jnp.concatenate([near, far], axis=1)
            hots.append(jnp.where(hot, 1.0, 0.0))
            if gates_too:
                gate_line = jnp.concatenate(lines(256, j), axis=1)
                gate_columns.append(jnp.sum(jnp.where(hot, gate_line, 0.0), axis=1, keepdims=True))
        if gates_too:
            column = jnp.concatenate(gate_columns, axis=0)
            gate_rows[g] = jnp.broadcast_to(column, (held * 2 * cap, 128))
        return jnp.dot(
            jnp.concatenate(hots, axis=0).astype(jnp.bfloat16), x, preferred_element_type=jnp.float32
        )

    def compute(g, theirs, ours):
        rows = [slice(j * 2 * cap, (j + 1) * 2 * cap) for j in range(held)]
        chosen = [
            jnp.concatenate([theirs[r], ours[r]], axis=0).astype(jnp.bfloat16) for r in rows
        ]
        for n in range(CHUNKS):
            for side in range(2):
                columns = slice(side * FF + n * chunk, side * FF + (n + 1) * chunk)
                here = slice(side * chunk, (side + 1) * chunk)
                parts = [
                    jnp.dot(chosen[j], weights[j, :, columns], preferred_element_type=jnp.float32)
                    for j in range(held)
                ]
                sent[g, n, :, here] = encode(
                    jnp.concatenate([p[: 2 * cap] for p in parts], axis=0), scale
                )
                mine[g, n, :, here] = jnp.concatenate([p[2 * cap :] for p in parts], axis=0)
            part_copy(g, n).start()

    def chip_of(step):
        zs, ys, _ = chip_at_step(step, z, y)
        return 2 * zs + ys

    def from_core(g, plane):
        unit_copy(g, 1 - k, plane, core_send.at[g * 2 + plane], core_peer).wait_recv()

    def forward(step):
        g = chip_of(step)
        for plane in (c, 1 - c):
            unit_copy(g, k, plane, core_send.at[g * 2 + plane], core_peer).wait_recv()
            each_send(step, plane, lambda copy: copy.start())

    def work(step, carry):
        @pl.when(step % 2 == 1)
        def _():
            forward(step)

            @pl.when(step < CHIPS - 1)
            def _():
                forward(step + 1)

        g = chip_of(step)
        from_core(g, c)
        from_core(g, 1 - c)
        ours = place(g, c, True)
        compute(g, place(g, 1 - c, False), ours)
        return carry

    each_send(0, c, lambda copy: copy.start())
    from_core(chip, c)
    ours = place(chip, c, True)
    for w in weight_loads:
        w.wait()
    x_rows(1 - c).wait_recv()
    x_table(1 - c).wait_recv()
    each_send(0, 1 - c, lambda copy: copy.start())
    from_core(chip, 1 - c)
    compute(chip, place(chip, 1 - c, False), ours)
    lax.fori_loop(1, CHIPS, work, 0)

    def finish(step, carry):
        zs, ys, _ = chip_at_step(step, z, y)
        g = 2 * zs + ys
        gate_column = gate_rows[g, :, 0:1]
        for plane in (c, 1 - c):
            each_send(step, plane, lambda copy: copy.wait_send())
        for n in range(CHUNKS):
            part_copy(g, n).wait_recv()
            first = mine[g, n, :, :chunk] + decode(got[g, n, :, :chunk], scale)
            second = mine[g, n, :, chunk:] + decode(got[g, n, :, chunk:], scale)
            hidden = first / (1.0 + jnp.exp(-first)) * second * gate_column
            for j in range(held):
                for core in range(2):
                    low = (j * 2 + core) * cap
                    out_ref[0, j, 2 * g + core, :, n * chunk : (n + 1) * chunk] = hidden[
                        low : low + cap
                    ].astype(jnp.bfloat16)
            part_copy(g, n).wait_send()
        return carry

    x_rows(c).wait_send()
    x_table(c).wait_send()
    lax.fori_loop(0, CHIPS, finish, 0)


def kernel_shards(moe_rows, expert_ids, expert_gates, expert_weights):
    sources = lax.axis_size("ep")
    tokens, width = moe_rows.shape
    held, half, columns = expert_weights.shape
    cap = max(2, 9 * tokens * TOP // (8 * sources * held))
    part_rows = held * 2 * cap
    scale = 2.0 ** math.floor(math.log2(49152.0 / (half * ROW_BOUND * WEIGHT_BOUND)))
    dma = pltpu.SemaphoreType.DMA
    vmem = pl.BlockSpec(memory_space=pltpu.VMEM)
    hbm = pl.BlockSpec(memory_space=pl.ANY)
    return pl.pallas_call(
        functools.partial(kernel, cap, scale),
        out_shape=pltpu.VMEM((1, held, sources, cap, columns // 2), jnp.bfloat16),
        in_specs=[hbm, hbm, hbm, hbm],
        out_specs=vmem,
        scratch_shapes=[
            pltpu.VMEM((CHIPS, 2, 2, tokens + META, half), jnp.bfloat16),
            pltpu.VMEM((held, half, columns), jnp.bfloat16),
            pltpu.VMEM((CHIPS, CHUNKS, part_rows, columns // CHUNKS), jnp.float32),
            pltpu.VMEM((CHIPS, CHUNKS, part_rows, columns // CHUNKS), jnp.bfloat16),
            pltpu.VMEM((CHIPS, CHUNKS, part_rows, columns // CHUNKS), jnp.bfloat16),
            pltpu.VMEM((CHIPS, part_rows, 128), jnp.float32),
            pltpu.VMEM((TOP, tokens), jnp.int32),
            pltpu.VMEM((TOP, tokens), jnp.bfloat16),
            dma,
            dma((2,)),
            dma((held,)),
            dma((2,)),
            dma((2,)),
            dma((2 * ZS,)),
            dma((2 * ZS,)),
            dma((2 * ZS,)),
            dma((2 * CHIPS,)),
            dma((4 * CHIPS,)),
            dma((CHIPS * CHUNKS,)),
            dma((CHIPS * CHUNKS,)),
        ],
        compiler_params=pltpu.CompilerParams(
            collective_id=0, has_side_effects=True, vmem_limit_bytes=56 * 1024 * 1024
        ),
        cost_estimate=pl.CostEstimate(
            flops=2 * CHIPS * held * 4 * cap * half * columns,
            bytes_accessed=held * half * columns * 2,
            transcendentals=0,
        ),
    )(moe_rows, expert_ids.T, expert_gates.T, expert_weights)


def solution(mesh):
    in_specs = (
        P(("ctx", "ep"), None),
        P(("ctx", "ep"), None),
        P(("ctx", "ep"), None),
        P("ep", "ctx", None),
    )
    out_specs = P("ctx", "ep", None, None, None)
    fits = mesh.shape["ctx"] == 2 and mesh.shape["ep"] == 2 * CHIPS
    body = kernel_shards if fits else general_shards
    return jax.shard_map(body, mesh=mesh, in_specs=in_specs, out_specs=out_specs, check_vma=False)
```

```python
import functools
import math

import jax
import jax.numpy as jnp
from jax import lax
from jax.experimental import pallas as pl
from jax.experimental.pallas import tpu as pltpu
from jax.sharding import PartitionSpec as P

FF = 768
TOP = 8
ROW_BOUND = 6.0
WEIGHT_BOUND = 0.125
META = 16
ZS = 4
CHIPS = 8
CHUNKS = 3


def place_rows(block_rows, block_ids, block_gates, experts, capacity):
    flat_ids = block_ids.reshape(-1)
    markers = (flat_ids[:, None] == jnp.arange(experts, dtype=jnp.int32)[None, :]).astype(jnp.int32)
    ranking = jnp.cumsum(markers, axis=0) - markers
    slot_index = jnp.sum(ranking * markers, axis=1)
    places = flat_ids * capacity + slot_index
    owners = jnp.arange(flat_ids.shape[0], dtype=jnp.int32) // block_ids.shape[1]
    buffer = (
        jnp.zeros((experts * capacity, block_rows.shape[1]), block_rows.dtype)
        .at[places]
        .set(block_rows[owners])
    )
    gate_buffer = (
        jnp.zeros((experts * capacity,), block_gates.dtype).at[places].set(block_gates.reshape(-1))
    )
    return (
        buffer.reshape(experts, capacity, block_rows.shape[1]),
        gate_buffer.reshape(experts, capacity),
    )


def project(inputs, weights):
    return jnp.einsum("sucd,udf->uscf", inputs, weights, preferred_element_type=jnp.float32)


def activate(before, gate_values):
    scaled = jnp.transpose(gate_values, (1, 0, 2)).astype(jnp.float32)[..., None]
    return (jax.nn.silu(before[..., :FF]) * before[..., FF:] * scaled).astype(jnp.bfloat16)


def general_shards(moe_rows, expert_ids, expert_gates, expert_weights):
    sources = lax.axis_size("ep")
    held_experts = expert_weights.shape[0]
    experts = sources * held_experts
    row_count = moe_rows.shape[0]
    capacity = max(2, 9 * row_count * TOP // (8 * experts))
    buffer, gate_buffer = place_rows(moe_rows, expert_ids, expert_gates, experts, capacity)
    buffer = buffer.reshape(sources, held_experts, capacity, buffer.shape[2])
    gate_buffer = gate_buffer.reshape(sources, held_experts, capacity)
    arrived, arrived_gates = (
        lax.all_to_all(buffer, "ep", split_axis=0, concat_axis=0, tiled=True),
        lax.all_to_all(gate_buffer, "ep", split_axis=0, concat_axis=0, tiled=True),
    )
    before = project(arrived, lax.all_gather(expert_weights, "ctx", axis=1, tiled=True))
    hidden = activate(before, arrived_gates)
    return hidden[None]


def chip_at_step(step, z, y):
    first, last, odd = (7 - step) // 7, step // 7, step % 2
    other = (1 - odd) * (1 - first) + last
    i = odd * ((step + 1) // 2) + (1 - odd) * (step // 2 - 1) + first - last
    mirror = z // 2
    inner = mirror * (ZS - 1 - z) + (1 - mirror) * z
    near = 1 - i // 2
    w = inner * (near * (1 - i) + (1 - near) * i) + (1 - inner) * i
    zs = mirror * (ZS - 1 - w) + (1 - mirror) * w
    ys = y + other * (1 - 2 * y)
    return zs, ys, other


def encode(p, scale):
    q = p * scale
    q2 = q * q
    q4 = q2 * q2
    q8 = q4 * q4
    return jnp.where(q < 0, -q8, q8).astype(jnp.bfloat16)


def decode(code, scale):
    v = code.astype(jnp.float32)
    size = jnp.exp(jnp.log(jnp.abs(v)) * 0.125) * (1.0 / scale)
    return jnp.where(v < 0, -size, size)


def kernel(
    cap, scale,
    rows_ref, ids_hbm, gates_hbm, weights_hbm, out_ref,
    blocks, weights, mine, sent, got, gate_rows,
    ids_ref, gates_ref, load_sem, small_sem, weight_sem, x_send, x_recv, up_send, down_send, y_send, core_send, unit_recv,
    part_send, part_recv,
):
    tokens, width = rows_ref.shape
    half = width // 2
    held = weights_hbm.shape[0]
    chunk = FF // CHUNKS
    c = lax.axis_index("ctx")
    e = lax.axis_index("ep")
    z, y, k = e // 4, (e // 2) % 2, e % 2
    chip = 2 * z + y
    x_peer = {"ctx": 1 - c, "ep": e}
    y_peer = {"ctx": c, "ep": 4 * z + 2 * (1 - y) + k}
    core_peer = {"ctx": c, "ep": 4 * z + 2 * y + 1 - k}
    up_peer = {"ctx": c, "ep": e + 4}
    down_peer = {"ctx": c, "ep": e - 4}
    not_top, not_bottom = z < ZS - 1, z > 0

    barrier = pltpu.get_barrier_semaphore()

    def greet(peer):
        pl.semaphore_signal(barrier, inc=1, device_id=peer, device_id_type=pl.DeviceIdType.MESH)

    greet(x_peer)
    greet(y_peer)
    greet(core_peer)

    @pl.when(not_top)
    def _():
        greet(up_peer)

    @pl.when(not_bottom)
    def _():
        greet(down_peer)

    load = pltpu.make_async_copy(
        rows_ref.at[:, pl.ds(pl.multiple_of(c * half, half), half)],
        blocks.at[chip, k, c, pl.ds(0, tokens)],
        load_sem,
    )
    small_loads = [
        pltpu.make_async_copy(ids_hbm, ids_ref, small_sem.at[0]),
        pltpu.make_async_copy(gates_hbm, gates_ref, small_sem.at[1]),
    ]
    for copy in small_loads:
        copy.start()
    load.start()
    weight_loads = [
        pltpu.make_async_copy(weights_hbm.at[j], weights.at[j], weight_sem.at[j]) for j in range(held)
    ]

    pl.semaphore_wait(barrier, 3 + (z + ZS - 1) // ZS + (2 * ZS - 2 - z) // ZS)

    def remote(src, dst, send_sem, recv_sem, peer):
        return pltpu.make_async_remote_copy(
            src_ref=src, dst_ref=dst, send_sem=send_sem, recv_sem=recv_sem,
            device_id=peer, device_id_type=pl.DeviceIdType.MESH,
        )

    def x_rows(plane):
        return remote(
            rows_ref.at[:, pl.ds(pl.multiple_of((1 - c) * half, half), half)],
            blocks.at[chip, k, plane, pl.ds(0, tokens)],
            x_send.at[0], x_recv.at[0], x_peer,
        )

    def x_table(plane):
        return remote(
            blocks.at[chip, k, plane, pl.ds(tokens, META), pl.ds(0, 512)],
            blocks.at[chip, k, plane, pl.ds(tokens, META), pl.ds(0, 512)],
            x_send.at[1], x_recv.at[1], x_peer,
        )

    x_rows(c).start()
    for copy in small_loads:
        copy.wait()

    expert = lax.broadcasted_iota(jnp.int32, (32, tokens), 0)
    ids = ids_ref[...]
    gates = gates_ref[...].astype(jnp.float32)
    marks = jnp.zeros((32, tokens), jnp.float32)
    gate_of = jnp.zeros((32, tokens), jnp.float32)
    for t in range(TOP):
        same = ids[t : t + 1] == expert
        marks = marks + jnp.where(same, 1.0, 0.0)
        gate_of = gate_of + jnp.where(same, gates[t : t + 1], 0.0)
    earlier = (
        lax.broadcasted_iota(jnp.int32, (tokens, tokens), 0)
        < lax.broadcasted_iota(jnp.int32, (tokens, tokens), 1)
    )
    rank = jnp.dot(
        marks.astype(jnp.bfloat16),
        jnp.where(earlier, 1.0, 0.0).astype(jnp.bfloat16),
        preferred_element_type=jnp.float32,
    )
    slots = jnp.where(marks > 0, rank, -1.0)
    table = jnp.concatenate(
        [slots[:16], slots[16:], gate_of[:16], gate_of[16:], jnp.zeros((META, half - 512), jnp.float32)],
        axis=1,
    )
    blocks[chip, k, c, tokens:, :] = table.astype(jnp.bfloat16)
    blocks[chip, k, 1 - c, tokens:, 512:] = jnp.zeros((META, half - 512), jnp.bfloat16)

    x_table(c).start()
    for w in weight_loads:
        w.start()
    load.wait()

    def unit_copy(g, core, plane, send_sem, peer):
        unit = blocks.at[g, core, plane]
        return remote(unit, unit, send_sem, unit_recv.at[(g * 2 + core) * 2 + plane], peer)

    def each_send(step, plane, act):
        zs, ys, other = chip_at_step(step, z, y)
        g = 2 * zs + ys

        act(unit_copy(g, k, plane, core_send.at[g * 2 + plane], core_peer))

        @pl.when((other == 0) & not_top & (zs <= z))
        def _():
            act(unit_copy(g, k, plane, up_send.at[zs * 2 + plane], up_peer))

        @pl.when((other == 0) & not_bottom & (zs >= z))
        def _():
            act(unit_copy(g, k, plane, down_send.at[zs * 2 + plane], down_peer))

        @pl.when(other == 0)
        def _():
            act(unit_copy(g, k, plane, y_send.at[zs * 2 + plane], y_peer))

    def part_copy(g, n):
        at = g * CHUNKS + n
        return remote(sent.at[g, n], got.at[g, n], part_send.at[at], part_recv.at[at], x_peer)

    def place(g, plane, gates_too):
        x = jnp.concatenate([blocks[g, core, plane, :tokens, :] for core in range(2)], axis=0)
        pick = lax.broadcasted_iota(jnp.int32, (META, 128), 0)
        row = lax.broadcasted_iota(jnp.int32, (2 * cap, 2 * tokens), 0).astype(jnp.float32)

        def lines(first, j):
            at = pl.multiple_of((e // 8) * 128 + first, 128)
            return [
                jnp.sum(
                    jnp.where(
                        pick == (e % 8) * 2 + j,
                        blocks[g, core, plane, tokens:, pl.ds(at, 128)].astype(jnp.float32),
                        0.0,
                    ),
                    axis=0,
                    keepdims=True,
                )
                for core in range(2)
            ]

        hots, gate_columns = [], []
        for j in range(held):
            near, far = lines(0, j)
            far = jnp.where(far >= 0, far + float(cap), -1.0)
            hot = row == jnp.concatenate([near, far], axis=1)
            hots.append(jnp.where(hot, 1.0, 0.0))
            if gates_too:
                gate_line = jnp.concatenate(lines(256, j), axis=1)
                gate_columns.append(jnp.sum(jnp.where(hot, gate_line, 0.0), axis=1, keepdims=True))
        if gates_too:
            column = jnp.concatenate(gate_columns, axis=0)
            gate_rows[g] = jnp.broadcast_to(column, (held * 2 * cap, 128))
        return jnp.dot(
            jnp.concatenate(hots, axis=0).astype(jnp.bfloat16), x, preferred_element_type=jnp.float32
        )

    def compute(g, theirs, ours):
        rows = [slice(j * 2 * cap, (j + 1) * 2 * cap) for j in range(held)]
        chosen = [
            jnp.concatenate([theirs[r], ours[r]], axis=0).astype(jnp.bfloat16) for r in rows
        ]
        for n in range(CHUNKS):
            kept = []
            for side in range(2):
                columns = slice(side * FF + n * chunk, side * FF + (n + 1) * chunk)
                here = slice(side * chunk, (side + 1) * chunk)
                parts = [
                    jnp.dot(chosen[j], weights[j, :, columns], preferred_element_type=jnp.float32)
                    for j in range(held)
                ]
                sent[g, n, :, here] = encode(
                    jnp.concatenate([p[: 2 * cap] for p in parts], axis=0), scale
                )
                kept.append((here, jnp.concatenate([p[2 * cap :] for p in parts], axis=0)))
            part_copy(g, n).start()
            for here, value in kept:
                mine[g, n, :, here] = value

    def chip_of(step):
        zs, ys, _ = chip_at_step(step, z, y)
        return 2 * zs + ys

    def from_core(g, plane):
        unit_copy(g, 1 - k, plane, core_send.at[g * 2 + plane], core_peer).wait_recv()

    def forward(step):
        g = chip_of(step)
        for plane in (c, 1 - c):
            unit_copy(g, k, plane, core_send.at[g * 2 + plane], core_peer).wait_recv()
            each_send(step, plane, lambda copy: copy.start())

    def work(step, carry):
        @pl.when(step % 2 == 1)
        def _():
            forward(step)

            @pl.when(step < CHIPS - 1)
            def _():
                forward(step + 1)

        g = chip_of(step)
        from_core(g, c)
        from_core(g, 1 - c)
        ours = place(g, c, True)
        compute(g, place(g, 1 - c, False), ours)
        return carry

    each_send(0, c, lambda copy: copy.start())
    from_core(chip, c)
    ours = place(chip, c, True)
    for w in weight_loads:
        w.wait()
    x_rows(1 - c).wait_recv()
    x_table(1 - c).wait_recv()
    each_send(0, 1 - c, lambda copy: copy.start())
    from_core(chip, 1 - c)
    compute(chip, place(chip, 1 - c, False), ours)
    lax.fori_loop(1, CHIPS, work, 0)

    def finish(step, carry):
        zs, ys, _ = chip_at_step(step, z, y)
        g = 2 * zs + ys
        gate_column = gate_rows[g, :, 0:1]
        for plane in (c, 1 - c):
            each_send(step, plane, lambda copy: copy.wait_send())
        for n in range(CHUNKS):
            part_copy(g, n).wait_recv()
            first = mine[g, n, :, :chunk] + decode(got[g, n, :, :chunk], scale)
            second = mine[g, n, :, chunk:] + decode(got[g, n, :, chunk:], scale)
            hidden = first / (1.0 + jnp.exp(-first)) * second * gate_column
            for j in range(held):
                for core in range(2):
                    low = (j * 2 + core) * cap
                    out_ref[0, j, 2 * g + core, :, n * chunk : (n + 1) * chunk] = hidden[
                        low : low + cap
                    ].astype(jnp.bfloat16)
            part_copy(g, n).wait_send()
        return carry

    x_rows(c).wait_send()
    x_table(c).wait_send()
    lax.fori_loop(0, CHIPS, finish, 0)


def kernel_shards(moe_rows, expert_ids, expert_gates, expert_weights):
    sources = lax.axis_size("ep")
    tokens, width = moe_rows.shape
    held, half, columns = expert_weights.shape
    cap = max(2, 9 * tokens * TOP // (8 * sources * held))
    part_rows = held * 2 * cap
    scale = 2.0 ** math.floor(math.log2(49152.0 / (half * ROW_BOUND * WEIGHT_BOUND)))
    dma = pltpu.SemaphoreType.DMA
    vmem = pl.BlockSpec(memory_space=pltpu.VMEM)
    hbm = pl.BlockSpec(memory_space=pl.ANY)
    return pl.pallas_call(
        functools.partial(kernel, cap, scale),
        out_shape=pltpu.VMEM((1, held, sources, cap, columns // 2), jnp.bfloat16),
        in_specs=[hbm, hbm, hbm, hbm],
        out_specs=vmem,
        scratch_shapes=[
            pltpu.VMEM((CHIPS, 2, 2, tokens + META, half), jnp.bfloat16),
            pltpu.VMEM((held, half, columns), jnp.bfloat16),
            pltpu.VMEM((CHIPS, CHUNKS, part_rows, columns // CHUNKS), jnp.float32),
            pltpu.VMEM((CHIPS, CHUNKS, part_rows, columns // CHUNKS), jnp.bfloat16),
            pltpu.VMEM((CHIPS, CHUNKS, part_rows, columns // CHUNKS), jnp.bfloat16),
            pltpu.VMEM((CHIPS, part_rows, 128), jnp.float32),
            pltpu.VMEM((TOP, tokens), jnp.int32),
            pltpu.VMEM((TOP, tokens), jnp.bfloat16),
            dma,
            dma((2,)),
            dma((held,)),
            dma((2,)),
            dma((2,)),
            dma((2 * ZS,)),
            dma((2 * ZS,)),
            dma((2 * ZS,)),
            dma((2 * CHIPS,)),
            dma((4 * CHIPS,)),
            dma((CHIPS * CHUNKS,)),
            dma((CHIPS * CHUNKS,)),
        ],
        compiler_params=pltpu.CompilerParams(
            collective_id=0, has_side_effects=True, vmem_limit_bytes=56 * 1024 * 1024
        ),
        cost_estimate=pl.CostEstimate(
            flops=2 * CHIPS * held * 4 * cap * half * columns,
            bytes_accessed=held * half * columns * 2,
            transcendentals=0,
        ),
    )(moe_rows, expert_ids.T, expert_gates.T, expert_weights)


def solution(mesh):
    in_specs = (
        P(("ctx", "ep"), None),
        P(("ctx", "ep"), None),
        P(("ctx", "ep"), None),
        P("ep", "ctx", None),
    )
    out_specs = P("ctx", "ep", None, None, None)
    fits = mesh.shape["ctx"] == 2 and mesh.shape["ep"] == 2 * CHIPS
    body = kernel_shards if fits else general_shards
    return jax.shard_map(body, mesh=mesh, in_specs=in_specs, out_specs=out_specs, check_vma=False)
```
